256 devices in a mesh: island: 16 (over x, z_lo, core), fsdp: 16 (over z_hi, y).
Axes of the slice: x: 4, y: 4, z: 8 (z_hi: 4, z_lo: 2; z = z_hi * 2 + z_lo), core: 2. Of those that a mesh axis runs over, the one named last changes fastest.
Arguments:
- pseudo_grads: float32 [16, 256, 28672], P('island', 'fsdp'), may hold values from -6 to 6
- master_slab: float32 [256, 28672], P('fsdp', 'island'), may hold values from -6 to 6
- momentum: float32 [256, 28672], P('fsdp', 'island'), may hold values from -3 to 3
- inner_inputs: bfloat16 [65536, 8192], P(('island', 'fsdp')), may hold values from -6 to 6
- token_ids: int32 [65536], P(('island', 'fsdp')), may hold values from 0 to 31999, as said below
- inner_weight: bfloat16 [16, 512, 8192], P('island', 'fsdp'), may hold values from -0.0625 to 0.0625
- readout: float32 [512], replicated, may hold values from -5 to 5
Outputs:
- new_slab: bfloat16 [256, 28672], P('fsdp')
- master_new: float32 [256, 28672], P('fsdp', 'island')
- momentum_new: float32 [256, 28672], P('fsdp', 'island')
- weight_grad: float32 [16, 512, 8192], P('island', 'fsdp')
- input_grad: bfloat16 [65536, 8192], P(('island', 'fsdp'))
The draws below stay inside these ranges and needn't reach their ends.
Inputs may be any that keep to these rules, and one draw needn't show every extreme that they name: `token_ids`: 0 marks a padding token; other values are token ids.
All inputs are finite; a program needn't handle non-finite values.
Results may differ from the reference program's by a relative error of at most 0.0049.
Values may be sent and summed in bfloat16 or wider, within the bound.
A program may use at most 128 MiB of HBM per device.

```python
import jax
import jax.numpy as jnp
from jax import lax

D = 8192
FF = 28672
VOCAB = 32000
R_OUT = 256
FF_IN = 512
TOK_DEV = 256
TOKENS = 65536
N_ISLAND = 16
N_FSDP = 16


def draw_token_ids(key, part):
    key = jax.random.fold_in(key, 7)
    first, second = jax.random.split(key)
    words = jax.random.randint(first, (TOKENS,), 1, VOCAB)
    padding = jax.random.randint(second, (TOKENS,), 0, 4)
    places = jnp.arange(TOKENS, dtype=jnp.int32)
    words = jnp.where(places == 1, VOCAB - 1, words)
    padding = jnp.where(places == TOKENS - 1, 0, jnp.where(places == 1, 1, padding))
    return jnp.where(padding == 0, 0, words).astype(jnp.int32)


def spiked(result, stream_key, source, target, shards_of, factor):
    owner, partner = [(jnp.arange(result.shape[axis_at]) // (result.shape[axis_at] // shards_of)).reshape([-1 if axis == axis_at else 1 for axis in range(result.ndim)]) for axis_at in (source, target)]
    chosen = jax.random.permutation(stream_key, shards_of)[partner]
    strong = (owner == chosen) | (owner == (partner + shards_of // 2) % shards_of)
    return jnp.where(strong, factor * result, result)


def levels(own_key, extent, shards, least, largest):
    level, own = 1.0, jax.random.fold_in(own_key, 6)
    for position, blocks in shards:
        steps = jnp.exp(jax.random.uniform(jax.random.fold_in(own, position), (blocks,), jnp.float32, least / len(shards), largest / len(shards)))
        level = level * jnp.repeat(steps, extent[position] // blocks).reshape([-1 if axis == position else 1 for axis in range(len(extent))])
    return level


def centred(stream_key, dims, spread, limit, pieces=(), kind=jnp.bfloat16):
    array = spread * jax.random.normal(stream_key, dims, jnp.float32)
    if pieces:
        array = array * levels(stream_key, dims, pieces, -0.22, 0.18)
    return jnp.clip(array, -limit, limit).astype(kind)


def noise_with(own_key, extent, spread, reach, cuts, heavy, kind=jnp.bfloat16):
    entries = spread * jax.random.normal(own_key, extent, jnp.float32)
    if cuts:
        entries = entries * levels(own_key, extent, cuts, -0.22, 0.18)
    return jnp.clip(spiked(entries, jax.random.fold_in(own_key, 3), *heavy), -reach, reach).astype(kind)


def setup_inputs(seed: int = 0) -> dict:
    streams_of = jax.random.split(jax.random.key(seed), 8)
    return {
        "pseudo_grads": noise_with(streams_of[0], (N_ISLAND, R_OUT, FF), 1.0, 6.0, ((0, 16), (1, 16)), (0, 2, 16, 2.0), jnp.float32),
        "master_slab": centred(streams_of[1], (R_OUT, FF), 1.0, 6.0, ((0, 16), (1, 16)), jnp.float32),
        "momentum": centred(streams_of[2], (R_OUT, FF), 0.5, 3.0, ((0, 16), (1, 16)), jnp.float32),
        "inner_inputs": centred(streams_of[3], (TOKENS, D), 1.0, 6.0, ((0, 256),)),
        "token_ids": draw_token_ids(jax.random.fold_in(streams_of[7], 71), 0),
        "inner_weight": centred(streams_of[5], (N_ISLAND, FF_IN, D), D ** -0.5, 0.0625, ((0, 16), (1, 16))),
        "readout": centred(streams_of[6], (FF_IN,), 1.0, 5.0, (), jnp.float32),
    }


def silu_slope(pre):
    sig = jax.nn.sigmoid(pre)
    return sig * (1.0 + pre * (1.0 - sig))

def island_pass(inputs, keep, weight, readout):
    island_tokens = inputs.shape[0]
    scale = 1.0 / jnp.sqrt(jnp.float32(island_tokens))
    blocks = island_tokens // TOK_DEV
    in_blocks = inputs.reshape(blocks, TOK_DEV, D)
    keep_blocks = keep.reshape(blocks, TOK_DEV)

    def one_block(grad_acc, items):
        block_in, block_keep = items
        pre = jnp.dot(block_in, weight.T, preferred_element_type=jnp.float32)
        slope = (scale * block_keep[:, None] * readout[None, :] * silu_slope(pre)).astype(jnp.bfloat16)
        grad_acc = grad_acc + jnp.dot(slope.T, block_in, preferred_element_type=jnp.float32)
        back = jnp.dot(slope, weight, preferred_element_type=jnp.float32).astype(jnp.bfloat16)
        return (grad_acc, back)
    start = jnp.zeros((FF_IN, D), jnp.float32)
    grad_acc, backs = lax.scan(one_block, start, (in_blocks, keep_blocks))
    return (grad_acc, backs.reshape(island_tokens, D))

def reference(pseudo_grads, master_slab, momentum, inner_inputs, token_ids, inner_weight, readout):
    mean_delta = lax.optimization_barrier(jnp.sum(pseudo_grads, axis=0)) / N_ISLAND
    momentum_new = 0.9 * momentum + mean_delta
    master_new = master_slab - 0.7 * (mean_delta + 0.9 * momentum_new)
    new_slab = master_new.astype(jnp.bfloat16)
    keep = (token_ids != 0).astype(jnp.float32)
    island_tokens = TOK_DEV * N_FSDP
    inputs_all = inner_inputs.reshape(N_ISLAND, island_tokens, D)
    keep_all = keep.reshape(N_ISLAND, island_tokens)

    def per_island(items):
        inputs, keep_rows, weight = items
        return island_pass(inputs, keep_rows, weight, readout)
    weight_grad, input_grad = lax.map(per_island, (inputs_all, keep_all, inner_weight))
    return (new_slab, master_new, momentum_new, weight_grad, input_grad.reshape(TOKENS, D))
```

```python
import math

import jax
import jax.numpy as jnp
from jax import lax
from jax.experimental import pallas as pl
from jax.experimental.pallas import tpu as pltpu
from jax.sharding import PartitionSpec as P

MESH = pl.DeviceIdType.MESH
F32, BF16 = jnp.float32, jnp.bfloat16
N_SEMS = 96


def kernel(
    groups, share, scale,
    pg, master, momentum, xin, tok, w, readout,
    slab_out, master_out, momentum_out, wg_out, dx_out,
    xb, wv, dwp, snd, slt, sl, dxb, tokb, rob, pre,
    ra1, ra0, rt1, rt0, ru1, ru0, rv1, rv0,
    acc, rc, rx, rz, msb, mob, slab,
    ssem, rsem, lsem, gsem,
):
    f, i = lax.axis_index("fsdp"), lax.axis_index("island")
    h, y = f // 4, lax.rem(f, 4)
    x, z, c = i // 4, lax.rem(i // 2, 2), lax.rem(i, 2)

    def at_y(d):
        return {"fsdp": h * 4 + lax.rem(y + d, 4)}

    def at_h(d):
        return {"fsdp": lax.rem(h + d, 4) * 4 + y}

    def at_x(d):
        return {"island": lax.rem(x + d, 4) * 4 + z * 2 + c}

    at_z = {"island": x * 4 + (1 - z) * 2 + c}
    at_c = {"island": x * 4 + z * 2 + 1 - c}

    k = xb.shape[1]
    r = w.shape[1]
    g = r * 4
    ka = share
    kb = k - ka
    ha, hb = ka // 2, kb // 2
    A, A1, A2 = pl.ds(0, ka), pl.ds(0, ha), pl.ds(ha, ha)
    B, B1, B2 = pl.ds(ka, kb), pl.ds(ka, hb), pl.ds(ka + hb, hb)

    def rows(dh, dy):
        return pl.ds(pl.multiple_of(dh * g + lax.rem(y + dy, 4) * r, r), r)

    def group(dh):
        return pl.ds(dh * g, g)

    copies = {}

    def send(name, src, dst, device):
        n = len(copies)
        copies[name] = pltpu.make_async_remote_copy(
            src_ref=src, dst_ref=dst, send_sem=ssem.at[n], recv_sem=rsem.at[n],
            device_id=device, device_id_type=MESH,
        )
        copies[name].start()

    def got(*names):
        for name in names:
            copies[name].wait_recv()

    loads = []

    def load(src, dst, n):
        cp = pltpu.make_async_copy(src, dst, lsem.at[n])
        cp.start()
        loads.append(cp)
        return cp

    cols = slab.shape[1] // groups

    def block(n):
        return pl.ds(pl.multiple_of(n * cols, 128), cols)

    lx = load(xin, xb, 0)
    lw = load(w.at[0], wv.at[rows(0, 0)], 1)
    lt = load(tok, tokb, 2)
    lr = load(readout, rob, 3)
    lms = load(master, msb, 4)
    lmo = load(momentum, mob, 5)
    for j in range(8):
        pltpu.make_async_copy(pg.at[0, :, block(2 * j + c)], acc.at[j], lsem.at[6]).start()

    barrier = pltpu.get_barrier_semaphore()
    partners = [at_y(1), at_y(3), at_h(1), at_h(3), at_x(1), at_x(2), at_x(3), at_z, at_c]
    for device in partners:
        pl.semaphore_signal(barrier, inc=1, device_id=device, device_id_type=MESH)
    pl.semaphore_wait(barrier, len(partners))

    own = rows(0, 0)
    send("Ah+", w.at[0, :, A], wv.at[rows(3, 0), A], at_h(1))
    send("Ah-", w.at[0, :, A], wv.at[rows(1, 0), A], at_h(3))
    send("By+", w.at[0, :, B], wv.at[own, B], at_y(1))
    send("By-", w.at[0, :, B], wv.at[own, B], at_y(3))
    send("Ay+0", w.at[0, :, A], wv.at[own, A], at_y(1))
    send("Ay-0", w.at[0, :, A], wv.at[own, A], at_y(3))
    for j in range(8):
        pltpu.make_async_remote_copy(
            src_ref=pg.at[0, :, block(2 * j + 1 - c)], dst_ref=rc.at[j], send_sem=gsem.at[0], recv_sem=gsem.at[1],
            device_id=at_c, device_id_type=MESH,
        ).start()

    def all_blocks(n, ref):
        return pltpu.make_async_remote_copy(
            src_ref=ref, dst_ref=ref, send_sem=gsem.at[n], recv_sem=gsem.at[n + 1], device_id=at_c, device_id_type=MESH
        )

    def pre_part(dh, lo, n, step, start):
        def body(j, total):
            at = pl.ds(pl.multiple_of(lo + j * step, 128), step)
            return total + lax.dot_general(
                wv[group(dh), at], xb[:, at], (((1,), (1,)), ((), ())), preferred_element_type=F32
            )

        return lax.fori_loop(0, n // step, body, start)

    def pre_a(dh):
        pre[group(dh)] = pre_part(dh, 0, ka, ka // 5, jnp.zeros((g, xb.shape[0]), F32))

    def slope(dh):
        p = pre_part(dh, ka, kb, kb, pre[group(dh)])
        sig = jax.nn.sigmoid(p)
        keep = (tokb[...] != 0).astype(F32)
        row = rob[pl.ds(lax.rem(h + dh, 4), 1), :]
        column = jnp.transpose(jnp.broadcast_to(row, (g, g)))
        weight = jnp.concatenate([column] * (xb.shape[0] // g), axis=1)
        s = scale * keep * weight * (sig * (1.0 + p * (1.0 - sig)))
        slt[group(dh)] = s.astype(BF16)
        sl[:, group(dh)] = jnp.transpose(s).astype(BF16)

    def dw(dh, lo, n, step):
        s = slt[group(dh)]

        def body(j, carry):
            at = pl.ds(pl.multiple_of(lo + j * step, 128), step)
            part = jnp.dot(s, xb[:, at], preferred_element_type=F32)
            dwp[group(dh), at] = part
            snd[group(dh), at] = part.astype(BF16)
            return carry

        lax.fori_loop(0, n // step, body, 0)

    def dw_all(dh):
        dw(dh, 0, ka, ka // 5)
        dw(dh, ka, kb, kb)

    def add(at_rows, lo, n, terms, step, keep=False, out=True):
        def body(j, carry):
            at = pl.ds(pl.multiple_of(lo + j * step, 128), step)
            total = dwp[at_rows, at]
            for ref, off in terms:
                total = total + ref[:, pl.ds(pl.multiple_of(lo - off + j * step, 128), step)].astype(F32)
            if keep:
                dwp[at_rows, at] = total
            if out:
                snd[at_rows, at] = total.astype(BF16)
            return carry

        lax.fori_loop(0, n // step, body, 0)

    sa, sb = ka // 10, kb // 2

    got("By+", "By-")
    send("Byf+", wv.at[rows(0, 3), B1], wv.at[rows(0, 3), B1], at_y(1))
    send("Byf-", wv.at[rows(0, 1), B2], wv.at[rows(0, 1), B2], at_y(3))

    pltpu.make_async_copy(acc, acc, lsem.at[6]).wait()
    all_blocks(0, rc).wait_recv()
    for j in range(8):
        acc[j] = acc[j] + rc[j]
    for d in (1, 3, 2):
        send(f"X{d}", acc.at[pl.ds(lax.rem(x + d, 4) * 2, 2)], rx.at[d - 1], at_x(d))

    got("Ay+0", "Ay-0")
    send("Ayf+0", wv.at[rows(0, 3), A1], wv.at[rows(0, 3), A1], at_y(1))
    send("Ayf-0", wv.at[rows(0, 1), A2], wv.at[rows(0, 1), A2], at_y(3))
    got("Byf+", "Byf-")
    lw.wait()

    got("Ah+", "Ah-")
    send("Ay+3", wv.at[rows(3, 0), A], wv.at[rows(3, 0), A], at_y(1))
    send("Ay-3", wv.at[rows(3, 0), A], wv.at[rows(3, 0), A], at_y(3))
    send("Ay+1", wv.at[rows(1, 0), A], wv.at[rows(1, 0), A], at_y(1))
    send("Ay-1", wv.at[rows(1, 0), A], wv.at[rows(1, 0), A], at_y(3))
    send("Ahf+", wv.at[rows(3, 0), A1], wv.at[rows(2, 0), A1], at_h(1))
    send("Ahf-", wv.at[rows(1, 0), A2], wv.at[rows(2, 0), A2], at_h(3))
    send("Bh+", wv.at[group(0), B], wv.at[group(3), B], at_h(1))
    send("Bh-", wv.at[group(0), B], wv.at[group(1), B], at_h(3))

    got("X1", "X3", "X2")
    two = acc.at[pl.ds(x * 2, 2)]
    two[...] = two[...] + rx[0] + rx[1] + rx[2]
    send("Z", acc.at[x * 2 + 1 - z], rz, at_z)

    got("Ayf+0", "Ayf-0")
    lx.wait()
    lt.wait()
    lr.wait()
    pre_a(0)
    slope(0)
    got("Ay+3", "Ay-3")
    send("Ayf+3", wv.at[rows(3, 3), A1], wv.at[rows(3, 3), A1], at_y(1))
    send("Ayf-3", wv.at[rows(3, 1), A2], wv.at[rows(3, 1), A2], at_y(3))
    got("Ahf+", "Ahf-")
    send("Ay+2", wv.at[rows(2, 0), A], wv.at[rows(2, 0), A], at_y(1))
    send("Ay-2", wv.at[rows(2, 0), A], wv.at[rows(2, 0), A], at_y(3))
    dw_all(0)

    got("Z")
    lms.wait()
    lmo.wait()
    mean = (acc[x * 2 + z] + rz[...]) / groups
    mob[...] = 0.9 * mob[...] + mean
    msb[...] = msb[...] - 0.7 * (mean + 0.9 * mob[...])
    mine = block(i)
    slab[:, mine] = msb[...].astype(BF16)
    send("SZ", slab.at[:, mine], slab.at[:, mine], at_z)
    load(msb, master_out, 7)
    load(mob, momentum_out, 8)

    got("Ay+1", "Ay-1")
    send("Ayf+1", wv.at[rows(1, 3), A1], wv.at[rows(1, 3), A1], at_y(1))
    send("Ayf-1", wv.at[rows(1, 1), A2], wv.at[rows(1, 1), A2], at_y(3))
    got("SZ")
    other = block(x * 4 + (1 - z) * 2 + c)
    for d in (1, 3, 2):
        send(f"SX{d}", slab.at[:, mine], slab.at[:, mine], at_x(d))
        send(f"SY{d}", slab.at[:, other], slab.at[:, other], at_x(d))
    got("Ayf+3", "Ayf-3")
    pre_a(3)
    got("Bh+", "Bh-")
    send("Bhf+", wv.at[group(3), B1], wv.at[group(2), B1], at_h(1))
    send("Bhf-", wv.at[group(1), B2], wv.at[group(2), B2], at_h(3))
    slope(3)
    got("Ayf+1", "Ayf-1")
    pre_a(1)
    got("Ay+2", "Ay-2")
    send("Ayf+2", wv.at[rows(2, 3), A1], wv.at[rows(2, 3), A1], at_y(1))
    send("Ayf-2", wv.at[rows(2, 1), A2], wv.at[rows(2, 1), A2], at_y(3))
    slope(1)
    dw_all(3)
    dw_all(1)
    got("SX1", "SX3", "SX2", "SY1", "SY3", "SY2")
    for j in range(8):
        at = block(2 * j + c)
        pltpu.make_async_remote_copy(
            src_ref=slab.at[:, at], dst_ref=slab.at[:, at], send_sem=gsem.at[2], recv_sem=gsem.at[3],
            device_id=at_c, device_id_type=MESH,
        ).start()

    def s1(d):
        send(f"S1+{d}", snd.at[rows(d, 2), A1], ra1.at[0, d], at_y(1))
        send(f"S1-{d}", snd.at[rows(d, 2), A2], ra1.at[1, d], at_y(3))

    def s2(d):
        send(f"S2+{d}", snd.at[rows(d, 1), A2], ra0.at[0, d, :, A2], at_y(1))
        send(f"S2-{d}", snd.at[rows(d, 3), A1], ra0.at[1, d, :, A1], at_y(3))

    def s3(d):
        got(f"S1+{d}", f"S1-{d}")
        add(rows(d, 1), 0, ha, [(ra1.at[0, d], 0)], sa)
        add(rows(d, 3), ha, ha, [(ra1.at[1, d], ha)], sa)
        send(f"S3+{d}", snd.at[rows(d, 1), A1], ra0.at[0, d, :, A1], at_y(1))
        send(f"S3-{d}", snd.at[rows(d, 3), A2], ra0.at[1, d, :, A2], at_y(3))

    def sum_a(d):
        got(f"S2+{d}", f"S2-{d}", f"S3+{d}", f"S3-{d}")
        add(rows(d, 0), 0, ka, [(ra0.at[0, d], 0), (ra0.at[1, d], 0)], sa, keep=True, out=d != 0)

    send("U2+", snd.at[group(1), B2], ru0.at[0, :, pl.ds(hb, hb)], at_h(1))
    send("U2-", snd.at[group(3), B1], ru0.at[1, :, pl.ds(0, hb)], at_h(3))
    s1(1)
    s1(3)
    got("Bhf+", "Bhf-")
    got("Ayf+2", "Ayf-2")
    pre_a(2)
    slope(2)
    dw_all(2)
    s1(2)
    s2(2)
    send("U1+", snd.at[group(2), B1], ru1.at[0], at_h(1))
    send("U1-", snd.at[group(2), B2], ru1.at[1], at_h(3))
    s2(1)
    s2(3)

    def dx(j, carry):
        at = pl.ds(pl.multiple_of(j * 512, 128), 512)
        dxb[:, at] = jnp.dot(sl[...], wv[:, at], preferred_element_type=F32).astype(BF16)
        return carry

    lax.fori_loop(0, k // 512, dx, 0)
    load(dxb, dx_out, 9)
    s3(2)
    s3(1)
    s3(3)
    s1(0)
    s2(0)
    got("U1+", "U1-")
    add(group(1), ka, hb, [(ru1.at[0], ka)], sb)
    add(group(3), ka + hb, hb, [(ru1.at[1], ka + hb)], sb)
    send("U3+", snd.at[group(1), B1], ru0.at[0, :, pl.ds(0, hb)], at_h(1))
    send("U3-", snd.at[group(3), B2], ru0.at[1, :, pl.ds(hb, hb)], at_h(3))
    all_blocks(2, slab.at[:, pl.ds(0, slab.shape[1] // 2)]).wait_recv()
    load(slab, slab_out, 10)
    sum_a(2)
    send("T1+", snd.at[rows(2, 0), A1], rt1.at[0], at_h(1))
    send("T1-", snd.at[rows(2, 0), A2], rt1.at[1], at_h(3))
    sum_a(1)
    send("T2+", snd.at[rows(1, 0), A2], rt0.at[0, :, A2], at_h(1))
    sum_a(3)
    send("T2-", snd.at[rows(3, 0), A1], rt0.at[1, :, A1], at_h(3))
    s3(0)
    got("U2+", "U2-", "U3+", "U3-")
    add(group(0), ka, kb, [(ru0.at[0], ka), (ru0.at[1], ka)], sb, keep=True)
    send("V1+", snd.at[rows(0, 2), B1], rv1.at[0], at_y(1))
    send("V1-", snd.at[rows(0, 2), B2], rv1.at[1], at_y(3))
    send("V2+", snd.at[rows(0, 1), B2], rv0.at[0, :, pl.ds(hb, hb)], at_y(1))
    send("V2-", snd.at[rows(0, 3), B1], rv0.at[1, :, pl.ds(0, hb)], at_y(3))
    got("T1+", "T1-")
    add(rows(1, 0), 0, ha, [(rt1.at[0], 0)], sa)
    add(rows(3, 0), ha, ha, [(rt1.at[1], ha)], sa)
    send("T3+", snd.at[rows(1, 0), A1], rt0.at[0, :, A1], at_h(1))
    send("T3-", snd.at[rows(3, 0), A2], rt0.at[1, :, A2], at_h(3))
    got("V1+", "V1-")
    add(rows(0, 1), ka, hb, [(rv1.at[0], ka)], sb)
    add(rows(0, 3), ka + hb, hb, [(rv1.at[1], ka + hb)], sb)
    send("V3+", snd.at[rows(0, 1), B1], rv0.at[0, :, pl.ds(0, hb)], at_y(1))
    send("V3-", snd.at[rows(0, 3), B2], rv0.at[1, :, pl.ds(hb, hb)], at_y(3))
    sum_a(0)
    got("V2+", "V2-", "V3+", "V3-")
    add(own, ka, kb, [(rv0.at[0], ka), (rv0.at[1], ka)], sb, keep=True, out=False)
    got("T2+", "T2-", "T3+", "T3-")
    add(own, 0, ka, [(rt0.at[0], 0), (rt0.at[1], 0)], sa, keep=True, out=False)
    load(dwp.at[own], wg_out.at[0], 11)

    for copy in copies.values():
        copy.wait_send()
    all_blocks(0, rc).wait_send()
    all_blocks(2, slab.at[:, pl.ds(0, slab.shape[1] // 2)]).wait_send()
    for cp in loads[6:]:
        cp.wait()


def on_device(pseudo_grads, master_slab, momentum, inner_inputs, token_ids, inner_weight, readout):
    groups = lax.axis_size("island")
    tokens, k = inner_inputs.shape
    r = inner_weight.shape[1]
    features = readout.shape[0]
    g = 4 * r
    width, cols = pseudo_grads.shape[2], master_slab.shape[1]
    out_rows = pseudo_grads.shape[1]
    share = (k // 256) * 25 // 32 * 256
    ka, kb = share, k - share
    ha, hb = ka // 2, kb // 2
    scale = 1.0 / math.sqrt(tokens * lax.axis_size("fsdp"))
    V, sem = pltpu.VMEM, pltpu.SemaphoreType.DMA
    anywhere = pl.BlockSpec(memory_space=pl.ANY)

    def body(*refs):
        kernel(groups, share, scale, *refs)

    return pl.pallas_call(
        body,
        out_shape=(
            jax.ShapeDtypeStruct((out_rows, width), BF16),
            jax.ShapeDtypeStruct(master_slab.shape, F32),
            jax.ShapeDtypeStruct(momentum.shape, F32),
            jax.ShapeDtypeStruct((1, r, k), F32),
            jax.ShapeDtypeStruct((tokens, k), BF16),
        ),
        in_specs=[anywhere] * 7,
        out_specs=[anywhere] * 5,
        scratch_shapes=[
            V((tokens, k), BF16),
            V((features, k), BF16),
            V((features, k), F32),
            V((features, k), BF16),
            V((features, tokens), BF16),
            V((tokens, features), BF16),
            V((tokens, k), BF16),
            V((1, tokens), jnp.int32),
            V((4, g), F32),
            V((features, tokens), F32),
            V((2, 4, r, ha), BF16),
            V((2, 4, r, ka), BF16),
            V((2, r, ha), BF16),
            V((2, r, ka), BF16),
            V((2, g, hb), BF16),
            V((2, g, kb), BF16),
            V((2, r, hb), BF16),
            V((2, r, kb), BF16),
            V((8, out_rows, cols), F32),
            V((8, out_rows, cols), F32),
            V((3, 2, out_rows, cols), F32),
            V((out_rows, cols), F32),
            V((out_rows, cols), F32),
            V((out_rows, cols), F32),
            V((out_rows, width), BF16),
            sem((N_SEMS,)),
            sem((N_SEMS,)),
            sem((12,)),
            sem((4,)),
        ],
        compiler_params=pltpu.CompilerParams(
            collective_id=0, has_side_effects=True, vmem_limit_bytes=63 * 2**20
        ),
        name="window",
    )(
        pseudo_grads, master_slab, momentum, inner_inputs, token_ids.reshape(1, tokens),
        inner_weight, readout.reshape(4, g),
    )


def solution(mesh):
    in_specs = (
        P("island", "fsdp", None),
        P("fsdp", "island"),
        P("fsdp", "island"),
        P(("island", "fsdp"), None),
        P(("island", "fsdp")),
        P("island", "fsdp", None),
        P(),
    )
    out_specs = (
        P("fsdp", None),
        P("fsdp", "island"),
        P("fsdp", "island"),
        P("island", "fsdp", None),
        P(("island", "fsdp"), None),
    )
    return jax.shard_map(
        on_device, mesh=mesh, in_specs=in_specs, out_specs=out_specs, check_vma=False
    )
```

```python
import math

import jax
import jax.numpy as jnp
from jax import lax
from jax.experimental import pallas as pl
from jax.experimental.pallas import tpu as pltpu
from jax.sharding import PartitionSpec as P

MESH = pl.DeviceIdType.MESH
F32, BF16 = jnp.float32, jnp.bfloat16
N_SEMS = 96


def kernel(
    groups, share, scale,
    pg, master, momentum, xin, tok, w, readout,
    slab, master_out, momentum_out, wg_out, dxb,
    xb, wv, dwp, snd, slt, sl, tokb, rob, pre,
    ra1, ra0, rt1, rt0, ru1, ru0, rv1, rv0,
    acc, rc, rx, rz, msb, mob,
    ssem, rsem, lsem, gsem,
):
    f, i = lax.axis_index("fsdp"), lax.axis_index("island")
    h, y = f // 4, lax.rem(f, 4)
    x, z, c = i // 4, lax.rem(i // 2, 2), lax.rem(i, 2)

    def at_y(d):
        return {"fsdp": h * 4 + lax.rem(y + d, 4)}

    def at_h(d):
        return {"fsdp": lax.rem(h + d, 4) * 4 + y}

    def at_x(d):
        return {"island": lax.rem(x + d, 4) * 4 + z * 2 + c}

    at_z = {"island": x * 4 + (1 - z) * 2 + c}
    at_c = {"island": x * 4 + z * 2 + 1 - c}

    k = xb.shape[1]
    r = w.shape[1]
    g = r * 4
    ka = share
    kb = k - ka
    ha, hb = ka // 2, kb // 2
    A, A1, A2 = pl.ds(0, ka), pl.ds(0, ha), pl.ds(ha, ha)
    B, B1, B2 = pl.ds(ka, kb), pl.ds(ka, hb), pl.ds(ka + hb, hb)

    def rows(dh, dy):
        return pl.ds(pl.multiple_of(dh * g + lax.rem(y + dy, 4) * r, r), r)

    def group(dh):
        return pl.ds(dh * g, g)

    copies = {}

    def send(name, src, dst, device):
        n = len(copies)
        copies[name] = pltpu.make_async_remote_copy(
            src_ref=src, dst_ref=dst, send_sem=ssem.at[n], recv_sem=rsem.at[n],
            device_id=device, device_id_type=MESH,
        )
        copies[name].start()

    def got(*names):
        for name in names:
            copies[name].wait_recv()

    loads = []

    def load(src, dst, n):
        cp = pltpu.make_async_copy(src, dst, lsem.at[n])
        cp.start()
        loads.append(cp)
        return cp

    cols = slab.shape[1] // groups

    def block(n):
        return pl.ds(pl.multiple_of(n * cols, 128), cols)

    lx = load(xin, xb, 0)
    lw = load(w.at[0], wv.at[rows(0, 0)], 1)
    lt = load(tok, tokb, 2)
    lr = load(readout, rob, 3)
    lms = load(master, msb, 4)
    lmo = load(momentum, mob, 5)
    for j in range(8):
        pltpu.make_async_copy(pg.at[0, :, block(2 * j + c)], acc.at[j], lsem.at[6]).start()

    barrier = pltpu.get_barrier_semaphore()
    partners = [at_y(1), at_y(3), at_h(1), at_h(3), at_x(1), at_x(2), at_x(3), at_z, at_c]
    for device in partners:
        pl.semaphore_signal(barrier, inc=1, device_id=device, device_id_type=MESH)
    pl.semaphore_wait(barrier, len(partners))

    own = rows(0, 0)
    send("Ah+", w.at[0, :, A], wv.at[rows(3, 0), A], at_h(1))
    send("Ah-", w.at[0, :, A], wv.at[rows(1, 0), A], at_h(3))
    send("By+", w.at[0, :, B], wv.at[own, B], at_y(1))
    send("By-", w.at[0, :, B], wv.at[own, B], at_y(3))
    send("Ay+0", w.at[0, :, A], wv.at[own, A], at_y(1))
    send("Ay-0", w.at[0, :, A], wv.at[own, A], at_y(3))
    for j in range(8):
        pltpu.make_async_remote_copy(
            src_ref=pg.at[0, :, block(2 * j + 1 - c)], dst_ref=rc.at[j], send_sem=gsem.at[0], recv_sem=gsem.at[1],
            device_id=at_c, device_id_type=MESH,
        ).start()

    def all_blocks(n, ref):
        return pltpu.make_async_remote_copy(
            src_ref=ref, dst_ref=ref, send_sem=gsem.at[n], recv_sem=gsem.at[n + 1], device_id=at_c, device_id_type=MESH
        )

    def pre_part(dh, lo, n, step, start):
        def body(j, total):
            at = pl.ds(pl.multiple_of(lo + j * step, 128), step)
            return total + lax.dot_general(
                wv[group(dh), at], xb[:, at], (((1,), (1,)), ((), ())), preferred_element_type=F32
            )

        return lax.fori_loop(0, n // step, body, start)

    def pre_a(dh):
        pre[group(dh)] = pre_part(dh, 0, ka, ka // 5, jnp.zeros((g, xb.shape[0]), F32))

    def slope(dh):
        p = pre_part(dh, ka, kb, kb, pre[group(dh)])
        sig = jax.nn.sigmoid(p)
        keep = (tokb[...] != 0).astype(F32)
        row = rob[pl.ds(lax.rem(h + dh, 4), 1), :]
        column = jnp.transpose(jnp.broadcast_to(row, (g, g)))
        weight = jnp.concatenate([column] * (xb.shape[0] // g), axis=1)
        s = scale * keep * weight * (sig * (1.0 + p * (1.0 - sig)))
        slt[group(dh)] = s.astype(BF16)
        sl[:, group(dh)] = jnp.transpose(s).astype(BF16)

    def dw(dh, lo, n, step):
        s = slt[group(dh)]

        def body(j, carry):
            at = pl.ds(pl.multiple_of(lo + j * step, 128), step)
            part = jnp.dot(s, xb[:, at], preferred_element_type=F32)
            dwp[group(dh), at] = part
            snd[group(dh), at] = part.astype(BF16)
            return carry

        lax.fori_loop(0, n // step, body, 0)

    def dw_all(dh):
        dw(dh, 0, ka, ka // 5)
        dw(dh, ka, kb, kb)

    def add(at_rows, lo, n, terms, step, keep=False, out=True, last=False):
        def body(j, carry):
            at = pl.ds(pl.multiple_of(lo + j * step, 128), step)
            total = dwp[at_rows, at]
            for ref, off in terms:
                total = total + ref[:, pl.ds(pl.multiple_of(lo - off + j * step, 128), step)].astype(F32)
            if last:
                wg_out[0, :, at] = total
            elif keep:
                dwp[at_rows, at] = total
            if out and not last:
                snd[at_rows, at] = total.astype(BF16)
            return carry

        lax.fori_loop(0, n // step, body, 0)

    sa, sb = ka // 10, kb // 2

    got("By+", "By-")
    send("Byf+", wv.at[rows(0, 3), B1], wv.at[rows(0, 3), B1], at_y(1))
    send("Byf-", wv.at[rows(0, 1), B2], wv.at[rows(0, 1), B2], at_y(3))

    pltpu.make_async_copy(acc, acc, lsem.at[6]).wait()
    all_blocks(0, rc).wait_recv()
    for j in range(8):
        acc[j] = acc[j] + rc[j]
    for d in (1, 3, 2):
        send(f"X{d}", acc.at[pl.ds(lax.rem(x + d, 4) * 2, 2)], rx.at[d - 1], at_x(d))

    got("Ay+0", "Ay-0")
    send("Ayf+0", wv.at[rows(0, 3), A1], wv.at[rows(0, 3), A1], at_y(1))
    send("Ayf-0", wv.at[rows(0, 1), A2], wv.at[rows(0, 1), A2], at_y(3))
    got("Byf+", "Byf-")
    lw.wait()

    got("Ah+", "Ah-")
    send("Ay+3", wv.at[rows(3, 0), A], wv.at[rows(3, 0), A], at_y(1))
    send("Ay-3", wv.at[rows(3, 0), A], wv.at[rows(3, 0), A], at_y(3))
    send("Ay+1", wv.at[rows(1, 0), A], wv.at[rows(1, 0), A], at_y(1))
    send("Ay-1", wv.at[rows(1, 0), A], wv.at[rows(1, 0), A], at_y(3))
    send("Ahf+", wv.at[rows(3, 0), A1], wv.at[rows(2, 0), A1], at_h(1))
    send("Ahf-", wv.at[rows(1, 0), A2], wv.at[rows(2, 0), A2], at_h(3))
    send("Bh+", wv.at[group(0), B], wv.at[group(3), B], at_h(1))
    send("Bh-", wv.at[group(0), B], wv.at[group(1), B], at_h(3))

    got("X1", "X3", "X2")
    two = acc.at[pl.ds(x * 2, 2)]
    two[...] = two[...] + rx[0] + rx[1] + rx[2]
    send("Z", acc.at[x * 2 + 1 - z], rz, at_z)

    got("Ayf+0", "Ayf-0")
    lx.wait()
    lt.wait()
    lr.wait()
    pre_a(0)
    slope(0)
    got("Ay+3", "Ay-3")
    send("Ayf+3", wv.at[rows(3, 3), A1], wv.at[rows(3, 3), A1], at_y(1))
    send("Ayf-3", wv.at[rows(3, 1), A2], wv.at[rows(3, 1), A2], at_y(3))
    got("Ahf+", "Ahf-")
    send("Ay+2", wv.at[rows(2, 0), A], wv.at[rows(2, 0), A], at_y(1))
    send("Ay-2", wv.at[rows(2, 0), A], wv.at[rows(2, 0), A], at_y(3))
    dw_all(0)

    got("Z")
    lms.wait()
    lmo.wait()
    mean = (acc[x * 2 + z] + rz[...]) / groups
    stepped = 0.9 * mob[...] + mean
    momentum_out[...] = stepped
    master_out[...] = msb[...] - 0.7 * (mean + 0.9 * stepped)
    mine = block(i)
    slab[:, mine] = master_out[...].astype(BF16)
    send("SZ", slab.at[:, mine], slab.at[:, mine], at_z)

    got("Ay+1", "Ay-1")
    send("Ayf+1", wv.at[rows(1, 3), A1], wv.at[rows(1, 3), A1], at_y(1))
    send("Ayf-1", wv.at[rows(1, 1), A2], wv.at[rows(1, 1), A2], at_y(3))
    got("SZ")
    other = block(x * 4 + (1 - z) * 2 + c)
    for d in (1, 3, 2):
        send(f"SX{d}", slab.at[:, mine], slab.at[:, mine], at_x(d))
        send(f"SY{d}", slab.at[:, other], slab.at[:, other], at_x(d))
    got("Ayf+3", "Ayf-3")
    pre_a(3)
    got("Bh+", "Bh-")
    send("Bhf+", wv.at[group(3), B1], wv.at[group(2), B1], at_h(1))
    send("Bhf-", wv.at[group(1), B2], wv.at[group(2), B2], at_h(3))
    slope(3)
    got("Ayf+1", "Ayf-1")
    pre_a(1)
    got("Ay+2", "Ay-2")
    send("Ayf+2", wv.at[rows(2, 3), A1], wv.at[rows(2, 3), A1], at_y(1))
    send("Ayf-2", wv.at[rows(2, 1), A2], wv.at[rows(2, 1), A2], at_y(3))
    slope(1)
    dw_all(3)
    dw_all(1)
    got("SX1", "SX3", "SX2", "SY1", "SY3", "SY2")
    for j in range(8):
        at = block(2 * j + c)
        pltpu.make_async_remote_copy(
            src_ref=slab.at[:, at], dst_ref=slab.at[:, at], send_sem=gsem.at[2], recv_sem=gsem.at[3],
            device_id=at_c, device_id_type=MESH,
        ).start()

    def s1(d):
        send(f"S1+{d}", snd.at[rows(d, 2), A1], ra1.at[0, d], at_y(1))
        send(f"S1-{d}", snd.at[rows(d, 2), A2], ra1.at[1, d], at_y(3))

    def s2(d):
        send(f"S2+{d}", snd.at[rows(d, 1), A2], ra0.at[0, d, :, A2], at_y(1))
        send(f"S2-{d}", snd.at[rows(d, 3), A1], ra0.at[1, d, :, A1], at_y(3))

    def s3(d):
        got(f"S1+{d}", f"S1-{d}")
        add(rows(d, 1), 0, ha, [(ra1.at[0, d], 0)], sa)
        add(rows(d, 3), ha, ha, [(ra1.at[1, d], ha)], sa)
        send(f"S3+{d}", snd.at[rows(d, 1), A1], ra0.at[0, d, :, A1], at_y(1))
        send(f"S3-{d}", snd.at[rows(d, 3), A2], ra0.at[1, d, :, A2], at_y(3))

    def sum_a(d):
        got(f"S2+{d}", f"S2-{d}", f"S3+{d}", f"S3-{d}")
        add(rows(d, 0), 0, ka, [(ra0.at[0, d], 0), (ra0.at[1, d], 0)], sa, keep=True, out=d != 0)

    send("U2+", snd.at[group(1), B2], ru0.at[0, :, pl.ds(hb, hb)], at_h(1))
    send("U2-", snd.at[group(3), B1], ru0.at[1, :, pl.ds(0, hb)], at_h(3))
    s1(1)
    s1(3)
    got("Bhf+", "Bhf-")
    got("Ayf+2", "Ayf-2")
    pre_a(2)
    slope(2)
    dw_all(2)
    s1(2)
    s2(2)
    send("U1+", snd.at[group(2), B1], ru1.at[0], at_h(1))
    send("U1-", snd.at[group(2), B2], ru1.at[1], at_h(3))
    s2(1)
    s2(3)

    def dx(j, carry):
        at = pl.ds(pl.multiple_of(j * 512, 128), 512)
        dxb[:, at] = jnp.dot(sl[...], wv[:, at], preferred_element_type=F32).astype(BF16)
        return carry

    lax.fori_loop(0, k // 512, dx, 0)
    s3(2)
    s3(1)
    s3(3)
    s1(0)
    s2(0)
    got("U1+", "U1-")
    add(group(1), ka, hb, [(ru1.at[0], ka)], sb)
    add(group(3), ka + hb, hb, [(ru1.at[1], ka + hb)], sb)
    send("U3+", snd.at[group(1), B1], ru0.at[0, :, pl.ds(0, hb)], at_h(1))
    send("U3-", snd.at[group(3), B2], ru0.at[1, :, pl.ds(hb, hb)], at_h(3))
    all_blocks(2, slab.at[:, pl.ds(0, slab.shape[1] // 2)]).wait_recv()
    sum_a(2)
    send("T1+", snd.at[rows(2, 0), A1], rt1.at[0], at_h(1))
    send("T1-", snd.at[rows(2, 0), A2], rt1.at[1], at_h(3))
    sum_a(1)
    send("T2+", snd.at[rows(1, 0), A2], rt0.at[0, :, A2], at_h(1))
    sum_a(3)
    send("T2-", snd.at[rows(3, 0), A1], rt0.at[1, :, A1], at_h(3))
    s3(0)
    got("U2+", "U2-", "U3+", "U3-")
    add(group(0), ka, kb, [(ru0.at[0], ka), (ru0.at[1], ka)], sb, keep=True)
    send("V1+", snd.at[rows(0, 2), B1], rv1.at[0], at_y(1))
    send("V1-", snd.at[rows(0, 2), B2], rv1.at[1], at_y(3))
    send("V2+", snd.at[rows(0, 1), B2], rv0.at[0, :, pl.ds(hb, hb)], at_y(1))
    send("V2-", snd.at[rows(0, 3), B1], rv0.at[1, :, pl.ds(0, hb)], at_y(3))
    got("T1+", "T1-")
    add(rows(1, 0), 0, ha, [(rt1.at[0], 0)], sa)
    add(rows(3, 0), ha, ha, [(rt1.at[1], ha)], sa)
    send("T3+", snd.at[rows(1, 0), A1], rt0.at[0, :, A1], at_h(1))
    send("T3-", snd.at[rows(3, 0), A2], rt0.at[1, :, A2], at_h(3))
    got("V1+", "V1-")
    add(rows(0, 1), ka, hb, [(rv1.at[0], ka)], sb)
    add(rows(0, 3), ka + hb, hb, [(rv1.at[1], ka + hb)], sb)
    send("V3+", snd.at[rows(0, 1), B1], rv0.at[0, :, pl.ds(0, hb)], at_y(1))
    send("V3-", snd.at[rows(0, 3), B2], rv0.at[1, :, pl.ds(hb, hb)], at_y(3))
    sum_a(0)
    got("V2+", "V2-", "V3+", "V3-")
    add(own, ka, kb, [(rv0.at[0], ka), (rv0.at[1], ka)], sb, last=True)
    got("T2+", "T2-", "T3+", "T3-")
    add(own, 0, ka, [(rt0.at[0], 0), (rt0.at[1], 0)], sa, last=True)

    for copy in copies.values():
        copy.wait_send()
    all_blocks(0, rc).wait_send()
    all_blocks(2, slab.at[:, pl.ds(0, slab.shape[1] // 2)]).wait_send()


def drain(*refs):
    sems = refs[-1]
    moves = [pltpu.make_async_copy(refs[n], refs[5 + n], sems.at[n]) for n in range(5)]
    for move in moves:
        move.start()
    for move in moves:
        move.wait()


def on_device(pseudo_grads, master_slab, momentum, inner_inputs, token_ids, inner_weight, readout):
    groups = lax.axis_size("island")
    tokens, k = inner_inputs.shape
    r = inner_weight.shape[1]
    features = readout.shape[0]
    g = 4 * r
    width, cols = pseudo_grads.shape[2], master_slab.shape[1]
    out_rows = pseudo_grads.shape[1]
    share = (k // 256) * 25 // 32 * 256
    ka, kb = share, k - share
    ha, hb = ka // 2, kb // 2
    scale = 1.0 / math.sqrt(tokens * lax.axis_size("fsdp"))
    V, sem = pltpu.VMEM, pltpu.SemaphoreType.DMA
    anywhere = pl.BlockSpec(memory_space=pl.ANY)

    def body(*refs):
        kernel(groups, share, scale, *refs)

    shapes = (
        ((out_rows, width), BF16),
        (master_slab.shape, F32),
        (momentum.shape, F32),
        ((1, r, k), F32),
        ((tokens, k), BF16),
    )
    results = pl.pallas_call(
        body,
        out_shape=tuple(V(*shape) for shape in shapes),
        in_specs=[anywhere] * 7,
        out_specs=[pl.BlockSpec(memory_space=pltpu.VMEM)] * 5,
        scratch_shapes=[
            V((tokens, k), BF16),
            V((features, k), BF16),
            V((features, k), F32),
            V((features, k), BF16),
            V((features, tokens), BF16),
            V((tokens, features), BF16),
            V((1, tokens), jnp.int32),
            V((4, g), F32),
            V((features, tokens), F32),
            V((2, 4, r, ha), BF16),
            V((2, 4, r, ka), BF16),
            V((2, r, ha), BF16),
            V((2, r, ka), BF16),
            V((2, g, hb), BF16),
            V((2, g, kb), BF16),
            V((2, r, hb), BF16),
            V((2, r, kb), BF16),
            V((8, out_rows, cols), F32),
            V((8, out_rows, cols), F32),
            V((3, 2, out_rows, cols), F32),
            V((out_rows, cols), F32),
            V((out_rows, cols), F32),
            V((out_rows, cols), F32),
            sem((N_SEMS,)),
            sem((N_SEMS,)),
            sem((12,)),
            sem((4,)),
        ],
        compiler_params=pltpu.CompilerParams(
            collective_id=0, has_side_effects=True, vmem_limit_bytes=54 * 2**20
        ),
        name="window",
    )(
        pseudo_grads, master_slab, momentum, inner_inputs, token_ids.reshape(1, tokens),
        inner_weight, readout.reshape(4, g),
    )
    return pl.pallas_call(
        drain,
        out_shape=tuple(jax.ShapeDtypeStruct(*shape) for shape in shapes),
        in_specs=[pl.BlockSpec(memory_space=pltpu.VMEM)] * 5,
        out_specs=[anywhere] * 5,
        scratch_shapes=[sem((5,))],
        compiler_params=pltpu.CompilerParams(vmem_limit_bytes=2**20),
        name="drain",
    )(*(pltpu.with_memory_space_constraint(result, pltpu.VMEM) for result in results))


def solution(mesh):
    in_specs = (
        P("island", "fsdp", None),
        P("fsdp", "island"),
        P("fsdp", "island"),
        P(("island", "fsdp"), None),
        P(("island", "fsdp")),
        P("island", "fsdp", None),
        P(),
    )
    out_specs = (
        P("fsdp", None),
        P("fsdp", "island"),
        P("fsdp", "island"),
        P("island", "fsdp", None),
        P(("island", "fsdp"), None),
    )
    return jax.shard_map(
        on_device, mesh=mesh, in_specs=in_specs, out_specs=out_specs, check_vma=False
    )
```

```python
import math

import jax
import jax.numpy as jnp
from jax import lax
from jax.experimental import pallas as pl
from jax.experimental.pallas import tpu as pltpu
from jax.sharding import PartitionSpec as P

MESH = pl.DeviceIdType.MESH
F32, BF16 = jnp.float32, jnp.bfloat16
N_SEMS = 144


def kernel(
    groups, share, back_share, scale,
    pg, master, momentum, xin, tok, w, readout,
    slab, master_out, momentum_out, wg_out, dxb,
    xo, xp, wv, dwp, snd, slt, slo, spt, sp, dxs, tokb, rob, preo, ps, pr,
    ra, rt1, rt0, ru1, ru0, rb, rs,
    acc, rc, rx, rz, msb, mob,
    ssem, rsem, lsem, gsem,
):
    f, i = lax.axis_index("fsdp"), lax.axis_index("island")
    h, y = f // 4, lax.rem(f, 4)
    x, z, c = i // 4, lax.rem(i // 2, 2), lax.rem(i, 2)

    mate = (y + 1 - 2 * lax.rem(y, 2), 3 - y)
    far = 3 - mate[0]
    n = xo.shape[1] // 2
    side = (lax.rem((y + 1) // 2, 2), y // 2)
    base = tuple(2 * n * q + n * side[q] for q in range(2))
    mate_base = tuple(2 * n * q + n * (1 - side[q]) for q in range(2))

    def at_y(d):
        return {"fsdp": h * 4 + d}

    def at_h(d):
        return {"fsdp": lax.rem(h + d, 4) * 4 + y}

    def at_x(d):
        return {"island": lax.rem(x + d, 4) * 4 + z * 2 + c}

    at_z = {"island": x * 4 + (1 - z) * 2 + c}
    at_c = {"island": x * 4 + z * 2 + 1 - c}
    pair = tuple(at_y(mate[q]) for q in range(2))
    link = (pair[1], pair[0])
    ways = (("+", at_h(1), 3, 1), ("-", at_h(3), 1, 3))

    r = w.shape[1]
    g = r * 4
    half = g // 2
    full = tuple(pl.ds(q * n, n) for q in range(2))
    ca, cb = share, n - share
    A = (pl.ds(0, ca), pl.ds(n + cb, ca))
    B = (pl.ds(ca, cb), pl.ds(n, cb))
    BB = pl.ds(ca, 2 * cb)
    sa, sb = back_share, n - back_share
    a_lo, b_lo = (0, n + sb), (sa, n)
    SA = (pl.ds(0, sa), pl.ds(n + sb, sa))
    SB = (pl.ds(sa, sb), pl.ds(n, sb))
    SBB = pl.ds(sa, 2 * sb)

    def rows(dh, at):
        return pl.ds(pl.multiple_of(dh * g + at * r, r), r)

    def group(dh):
        return pl.ds(dh * g, g)

    def low(dh):
        return pl.ds(dh * g, half)

    def high(dh):
        return pl.ds(dh * g + half, half)

    def wide(start, size):
        return pl.ds(pl.multiple_of(start, 128), size)

    def own_w(q, lo, size):
        return w.at[0, :, wide(base[q] + lo - q * n, size)]

    copies = {}

    def send(name, src, dst, device):
        k = len(copies)
        copies[name] = pltpu.make_async_remote_copy(
            src_ref=src, dst_ref=dst, send_sem=ssem.at[k], recv_sem=rsem.at[k],
            device_id=device, device_id_type=MESH,
        )
        copies[name].start()

    def got(*names):
        for name in names:
            copies[name].wait_recv()

    def got_both(*names):
        for name in names:
            got(name + "0", name + "1")

    def got_ways(*names):
        for name in names:
            got(name + "+", name + "-")

    def load(src, dst, k):
        cp = pltpu.make_async_copy(src, dst, lsem.at[k])
        cp.start()
        return cp

    cols = slab.shape[1] // groups

    def block(k):
        return wide(k * cols, cols)

    mine_rows = rows(0, y)
    lw = [load(own_w(q, q * n, n), wv.at[mine_rows, full[q]], q) for q in range(2)]
    lx = [load(xin.at[:, wide(base[q], n)], xo.at[:, full[q]], 2 + q) for q in range(2)]
    small = [load(tok, tokb, 4), load(readout, rob, 5)]
    states = [load(master, msb, 6), load(momentum, mob, 7)]
    for j in range(8):
        pltpu.make_async_copy(pg.at[0, :, block(2 * j + c)], acc.at[j], lsem.at[8]).start()

    barrier = pltpu.get_barrier_semaphore()
    partners = [pair[0], pair[1], at_h(1), at_h(3), at_x(1), at_x(2), at_x(3), at_z, at_c]
    for device in partners:
        pl.semaphore_signal(barrier, inc=1, device_id=device, device_id_type=MESH)
    pl.semaphore_wait(barrier, len(partners))

    for q in range(2):
        send(f"w{q}", w.at[0, :, wide(mate_base[q], n)], wv.at[mine_rows, full[q]], pair[q])
    for q in range(2):
        for s, device, slot, _ in ways:
            send(f"wa{q}o{s}", own_w(q, A[q].start, ca), wv.at[rows(slot, y), A[q]], device)
    for q in range(2):
        send(f"ybo{q}", own_w(q, B[q].start, cb), wv.at[mine_rows, B[q]], link[q])
        send(f"ya0o{q}", own_w(q, A[q].start, ca), wv.at[mine_rows, A[q]], link[q])
    for j in range(8):
        pltpu.make_async_remote_copy(
            src_ref=pg.at[0, :, block(2 * j + 1 - c)], dst_ref=rc.at[j], send_sem=gsem.at[0], recv_sem=gsem.at[1],
            device_id=at_c, device_id_type=MESH,
        ).start()

    def all_blocks(k, ref):
        return pltpu.make_async_remote_copy(
            src_ref=ref, dst_ref=ref, send_sem=gsem.at[k], recv_sem=gsem.at[k + 1], device_id=at_c, device_id_type=MESH
        )

    def product(at_rows, xs, lo, size):
        def body(j, total):
            at = wide(lo + j * (n // 2), n // 2)
            return total + lax.dot_general(
                wv[at_rows, at], xs[:, at], (((1,), (1,)), ((), ())), preferred_element_type=F32
            )

        return lax.fori_loop(0, size // (n // 2), body, jnp.zeros((g, xs.shape[0]), F32))

    def pre(d):
        for q in range(2):
            ps[q, group(d)] = product(group(d), xp, q * n, n)
            send(f"p{d}{q}", ps.at[q, group(d)], pr.at[q, group(d)], pair[q])
        preo[group(d)] = product(group(d), xo, 0, 2 * n)

    def slope(d):
        got_both(f"p{d}")
        p = preo[group(d)] + pr[0, group(d)] + pr[1, group(d)]
        sig = jax.nn.sigmoid(p)
        keep = (tokb[...] != 0).astype(F32)
        row = rob[pl.ds(lax.rem(h + d, 4), 1), :]
        column = jnp.transpose(jnp.broadcast_to(row, (g, g)))
        weight = jnp.concatenate([column] * (p.shape[1] // g), axis=1)
        value = scale * keep * weight * (sig * (1.0 + p * (1.0 - sig)))
        slt[group(d)] = value.astype(BF16)
        for q in range(2):
            send(f"s{d}{q}", slt.at[group(d)], spt.at[q, group(d)], pair[q])
        slo[:, group(d)] = jnp.transpose(value).astype(BF16)

    def dw(d):
        got_both(f"s{d}")
        own = slt[group(d)]
        for q in range(2):
            other = spt[q, group(d)]

            def body(j, carry, q=q, other=other):
                at = wide(q * n + j * (n // 2), n // 2)
                part = jnp.dot(own, xo[:, at], preferred_element_type=F32) + jnp.dot(
                    other, xp[:, at], preferred_element_type=F32
                )
                dwp[group(d), at] = part
                snd[group(d), at] = part.astype(BF16)
                return carry

            lax.fori_loop(0, 2, body, 0)

    def turn(d):
        for q in range(2):
            sp[q, :, group(d)] = jnp.transpose(spt[q, group(d)].astype(F32)).astype(BF16)

    def add(at_rows, lo, size, terms, to=None):
        units = size // 128
        step = 128 * max(k for k in range(1, 6) if units % k == 0)

        def body(j, carry):
            at = wide(lo + j * step, step)
            there = wide(j * step, step)
            total = dwp[at_rows, at]
            for ref in terms:
                total = total + ref[:, there].astype(F32)
            if to != "snd":
                dwp[at_rows, at] = total
            if to != "dwp":
                snd[at_rows, at] = total.astype(BF16)
            return carry

        lax.fori_loop(0, size // step, body, 0)

    def across(d, at):
        for q in range(2):
            part = wv.at[rows(d, y if at == "o" else mate[q]), A[q]]
            send(f"ya{d}{at}{q}", part, part, link[q])

    got_both("w")
    for q in range(2):
        part = wv.at[rows(0, mate[q]), B[q]]
        send(f"ybm{q}", part, part, link[q])
    across(0, "m")
    for q in range(2):
        for s, device, slot, _ in ways:
            send(f"wa{q}m{s}", wv.at[rows(0, mate[q]), A[q]], wv.at[rows(slot, mate[q]), A[q]], device)
    for q in range(2):
        send(f"x{q}", xin.at[:, wide(mate_base[q], n)], xp.at[:, full[q]], pair[q])
    got_both("ybo", "ybm")
    lw[0].wait()
    lw[1].wait()
    for s, device, slot, _ in ways:
        send(f"hb{s}", wv.at[group(0), BB], wv.at[group(slot), BB], device)
    got_ways("wa0o", "wa1o")
    for q in range(2):
        send(f"wf{q}+", wv.at[rows(3, y), A[q]], wv.at[rows(2, y), A[q]], at_h(1))
    across(3, "o")
    across(1, "o")
    got_ways("wa0m", "wa1m")
    for q in range(2):
        send(f"wf{q}-", wv.at[rows(1, mate[q]), A[q]], wv.at[rows(2, mate[q]), A[q]], at_h(3))
    across(3, "m")
    across(1, "m")

    pltpu.make_async_copy(acc, acc, lsem.at[8]).wait()
    all_blocks(0, rc).wait_recv()
    for j in range(8):
        acc[j] = acc[j] + rc[j]
    for d in (1, 3, 2):
        send(f"X{d}", acc.at[pl.ds(lax.rem(x + d, 4) * 2, 2)], rx.at[d - 1], at_x(d))
    got("X1", "X3", "X2")
    two = acc.at[pl.ds(x * 2, 2)]
    two[...] = two[...] + rx[0] + rx[1] + rx[2]
    send("Z", acc.at[x * 2 + 1 - z], rz, at_z)

    for cp in lx + small + states:
        cp.wait()
    got_both("ya0o", "ya0m", "x")
    pre(0)
    got_ways("hb")
    send("hbf+", wv.at[low(3), BB], wv.at[low(2), BB], at_h(1))
    send("hbf-", wv.at[high(1), BB], wv.at[high(2), BB], at_h(3))
    got_both("ya3o", "ya3m")
    pre(3)
    got_ways("wf0", "wf1")
    across(2, "o")
    across(2, "m")
    got_both("ya1o", "ya1m")
    pre(1)
    slope(0)

    got("Z")
    mean = (acc[x * 2 + z] + rz[...]) / groups
    stepped = 0.9 * mob[...] + mean
    momentum_out[...] = stepped
    master_out[...] = msb[...] - 0.7 * (mean + 0.9 * stepped)
    mine = block(i)
    slab[:, mine] = master_out[...].astype(BF16)
    send("SZ", slab.at[:, mine], slab.at[:, mine], at_z)

    slope(3)
    slope(1)
    got_both("ya2o", "ya2m")
    got_ways("hbf")
    pre(2)
    dw(0)
    dw(3)
    dw(1)

    def across_back(d):
        for q in range(2):
            for k, at in enumerate((mate[1 - q], far)):
                send(f"sa{d}{k}{q}", snd.at[rows(d, at), SA[q]], ra.at[q, d, k], link[q])

    def sum_across(d, to=None):
        got_both(f"sa{d}0", f"sa{d}1")
        for q in range(2):
            add(rows(d, y), a_lo[q], sa, [ra.at[q, d, 0]], to)
            add(rows(d, mate[q]), a_lo[q], sa, [ra.at[q, d, 1]], to)

    send("U2+", snd.at[high(1), SBB], ru0.at[0, pl.ds(half, half)], at_h(1))
    send("U2-", snd.at[low(3), SBB], ru0.at[1, pl.ds(0, half)], at_h(3))
    across_back(1)
    slope(2)
    across_back(3)
    got("SZ")
    other = block(x * 4 + (1 - z) * 2 + c)
    for d in (1, 3, 2):
        send(f"SX{d}", slab.at[:, mine], slab.at[:, mine], at_x(d))
        send(f"SY{d}", slab.at[:, other], slab.at[:, other], at_x(d))
    for d in (0, 3, 1):
        turn(d)
    dw(2)
    send("U1+", snd.at[low(2), SBB], ru1.at[0], at_h(1))
    send("U1-", snd.at[high(2), SBB], ru1.at[1], at_h(3))
    across_back(2)
    across_back(0)
    turn(2)

    def dx_mate(q):
        def body(j, carry):
            at = wide(q * n + j * (n // 4), n // 4)
            dxs[:, at] = jnp.dot(sp[q], wv[:, at], preferred_element_type=F32).astype(BF16)
            return carry

        lax.fori_loop(0, 4, body, 0)
        send(f"dx{q}", dxs.at[:, full[q]], dxb.at[:, wide(base[q], n)], pair[q])

    sum_across(1)
    for q in range(2):
        send(f"T2{q}+", snd.at[rows(1, mate[q]), SA[q]], rt0.at[q, 0, 1], at_h(1))
    dx_mate(0)
    sum_across(3)
    for q in range(2):
        send(f"T2{q}-", snd.at[rows(3, y), SA[q]], rt0.at[q, 1, 0], at_h(3))
    dx_mate(1)

    sum_across(2)
    for q in range(2):
        send(f"T1{q}+", snd.at[rows(2, y), SA[q]], rt1.at[q, 0], at_h(1))
        send(f"T1{q}-", snd.at[rows(2, mate[q]), SA[q]], rt1.at[q, 1], at_h(3))
    got_ways("U1")
    add(low(1), SBB.start, 2 * sb, [ru1.at[0]], "snd")
    add(high(3), SBB.start, 2 * sb, [ru1.at[1]], "snd")
    send("U3+", snd.at[low(1), SBB], ru0.at[0, pl.ds(0, half)], at_h(1))
    send("U3-", snd.at[high(3), SBB], ru0.at[1, pl.ds(half, half)], at_h(3))
    got("SX1", "SX3", "SX2", "SY1", "SY3", "SY2")
    for j in range(8):
        at = block(2 * j + c)
        pltpu.make_async_remote_copy(
            src_ref=slab.at[:, at], dst_ref=slab.at[:, at], send_sem=gsem.at[2], recv_sem=gsem.at[3],
            device_id=at_c, device_id_type=MESH,
        ).start()
    for q in range(2):
        got_ways(f"T1{q}")
        add(rows(1, y), a_lo[q], sa, [rt1.at[q, 0]], "snd")
        add(rows(3, mate[q]), a_lo[q], sa, [rt1.at[q, 1]], "snd")
        send(f"T3{q}+", snd.at[rows(1, y), SA[q]], rt0.at[q, 0, 0], at_h(1))
        send(f"T3{q}-", snd.at[rows(3, mate[q]), SA[q]], rt0.at[q, 1, 1], at_h(3))
    for q in range(2):

        def dx_own(j, carry, q=q):
            at = wide(q * n + j * (n // 4), n // 4)
            there = wide(base[q] + j * (n // 4), n // 4)
            dxb[:, there] = jnp.dot(slo[...], wv[:, at], preferred_element_type=F32).astype(BF16)
            return carry

        lax.fori_loop(0, 4, dx_own, 0)
    sum_across(0, "dwp")
    got_ways("U2", "U3")
    add(group(0), SBB.start, 2 * sb, [ru0.at[0], ru0.at[1]])
    for q in range(2):
        for k, at in enumerate((mate[1 - q], far)):
            send(f"sb{k}{q}", snd.at[rows(0, at), SB[q]], rb.at[q, k], link[q])
    got_both("sb0", "sb1")
    for q in range(2):
        add(mine_rows, b_lo[q], sb, [rb.at[q, 0]], "dwp")
        add(rows(0, mate[q]), b_lo[q], sb, [rb.at[q, 1]], "snd")
        send(f"fb{q}", snd.at[rows(0, mate[q]), SB[q]], rs.at[q, :, pl.ds(b_lo[q] - q * n, sb)], pair[q])
    for q in range(2):
        got_ways(f"T2{q}", f"T3{q}")
        add(rows(0, mate[q]), a_lo[q], sa, [rt0.at[q, 0, 1], rt0.at[q, 1, 1]], "snd")
        send(f"fa{q}", snd.at[rows(0, mate[q]), SA[q]], rs.at[q, :, pl.ds(a_lo[q] - q * n, sa)], pair[q])
    for q in range(2):
        add(mine_rows, a_lo[q], sa, [rt0.at[q, 0, 0], rt0.at[q, 1, 0]], "dwp")
        wg_out[0, :, wide(base[q], n)] = dwp[mine_rows, full[q]]
    for q in range(2):
        got(f"fa{q}", f"fb{q}")
        wg_out[0, :, wide(mate_base[q], n)] = rs[q].astype(F32)
    got_both("dx")
    all_blocks(2, slab.at[:, pl.ds(0, slab.shape[1] // 2)]).wait_recv()

    for copy in copies.values():
        copy.wait_send()
    all_blocks(0, rc).wait_send()
    all_blocks(2, slab.at[:, pl.ds(0, slab.shape[1] // 2)]).wait_send()


def drain(*refs):
    sems = refs[-1]
    moves = [pltpu.make_async_copy(refs[n], refs[5 + n], sems.at[n]) for n in range(5)]
    for move in moves:
        move.start()
    for move in moves:
        move.wait()


def on_device(pseudo_grads, master_slab, momentum, inner_inputs, token_ids, inner_weight, readout):
    groups = lax.axis_size("island")
    tokens, k = inner_inputs.shape
    r = inner_weight.shape[1]
    features = readout.shape[0]
    g = 4 * r
    width, cols = pseudo_grads.shape[2], master_slab.shape[1]
    out_rows = pseudo_grads.shape[1]
    n = k // 4
    share, back_share = 9 * n // 16, 12 * n // 16
    sa, sb = back_share, n - back_share
    scale = 1.0 / math.sqrt(tokens * lax.axis_size("fsdp"))
    V, sem = pltpu.VMEM, pltpu.SemaphoreType.DMA
    anywhere = pl.BlockSpec(memory_space=pl.ANY)

    def body(*refs):
        kernel(groups, share, back_share, scale, *refs)

    shapes = (
        ((out_rows, width), BF16),
        (master_slab.shape, F32),
        (momentum.shape, F32),
        ((1, r, k), F32),
        ((tokens, k), BF16),
    )
    results = pl.pallas_call(
        body,
        out_shape=tuple(V(*shape) for shape in shapes),
        in_specs=[anywhere] * 7,
        out_specs=[pl.BlockSpec(memory_space=pltpu.VMEM)] * 5,
        scratch_shapes=[
            V((tokens, 2 * n), BF16),
            V((tokens, 2 * n), BF16),
            V((features, 2 * n), BF16),
            V((features, 2 * n), F32),
            V((features, 2 * n), BF16),
            V((features, tokens), BF16),
            V((tokens, features), BF16),
            V((2, features, tokens), BF16),
            V((2, tokens, features), BF16),
            V((tokens, 2 * n), BF16),
            V((1, tokens), jnp.int32),
            V((4, g), F32),
            V((features, tokens), F32),
            V((2, features, tokens), F32),
            V((2, features, tokens), F32),
            V((2, 4, 2, r, sa), BF16),
            V((2, 2, r, sa), BF16),
            V((2, 2, 2, r, sa), BF16),
            V((2, g // 2, 2 * sb), BF16),
            V((2, g, 2 * sb), BF16),
            V((2, 2, r, sb), BF16),
            V((2, r, n), BF16),
            V((8, out_rows, cols), F32),
            V((8, out_rows, cols), F32),
            V((3, 2, out_rows, cols), F32),
            V((out_rows, cols), F32),
            V((out_rows, cols), F32),
            V((out_rows, cols), F32),
            sem((N_SEMS,)),
            sem((N_SEMS,)),
            sem((12,)),
            sem((4,)),
        ],
        compiler_params=pltpu.CompilerParams(
            collective_id=0, has_side_effects=True, vmem_limit_bytes=54 * 2**20
        ),
        name="window",
    )(
        pseudo_grads, master_slab, momentum, inner_inputs, token_ids.reshape(1, tokens),
        inner_weight, readout.reshape(4, g),
    )
    return pl.pallas_call(
        drain,
        out_shape=tuple(jax.ShapeDtypeStruct(*shape) for shape in shapes),
        in_specs=[pl.BlockSpec(memory_space=pltpu.VMEM)] * 5,
        out_specs=[anywhere] * 5,
        scratch_shapes=[sem((5,))],
        compiler_params=pltpu.CompilerParams(vmem_limit_bytes=2**20),
        name="drain",
    )(*(pltpu.with_memory_space_constraint(result, pltpu.VMEM) for result in results))


def solution(mesh):
    in_specs = (
        P("island", "fsdp", None),
        P("fsdp", "island"),
        P("fsdp", "island"),
        P(("island", "fsdp"), None),
        P(("island", "fsdp")),
        P("island", "fsdp", None),
        P(),
    )
    out_specs = (
        P("fsdp", None),
        P("fsdp", "island"),
        P("fsdp", "island"),
        P("island", "fsdp", None),
        P(("island", "fsdp"), None),
    )
    return jax.shard_map(
        on_device, mesh=mesh, in_specs=in_specs, out_specs=out_specs, check_vma=False
    )
```

```python
import math

import jax
import jax.numpy as jnp
from jax import lax
from jax.experimental import pallas as pl
from jax.experimental.pallas import tpu as pltpu
from jax.sharding import PartitionSpec as P

MESH = pl.DeviceIdType.MESH
F32, BF16 = jnp.float32, jnp.bfloat16
N_SEMS = 96


def kernel(
    groups, share, back_share, scale,
    pg, master, momentum, xin, tok, w, readout,
    slab, master_out, momentum_out, wg_out, dxb,
    xo, xp, wv, dwp, snd, slt, slo, spt, sp, dxs, tokb, rob, preo, ps, pr,
    ra, rt1, rt0, ru1, ru0, rb, rs,
    acc, rc, rx, rz, msb, mob,
    ssem, rsem, lsem, gsem,
):
    f, i = lax.axis_index("fsdp"), lax.axis_index("island")
    h, y = f // 4, lax.rem(f, 4)
    x, z, c = i // 4, lax.rem(i // 2, 2), lax.rem(i, 2)

    one, two = y + 1 - 2 * lax.rem(y, 2), 3 - y
    mate = one + c * (two - one)
    near = two + c * (one - two)
    far = 3 - one
    n = xo.shape[1]
    side = lax.rem((y + 1) // 2, 2) * (1 - c) + (y // 2) * c
    base, mate_base = n * side, n * (1 - side)

    def at_y(d):
        return {"fsdp": h * 4 + d}

    def at_h(d):
        return {"fsdp": lax.rem(h + d, 4) * 4 + y}

    def at_x(d):
        return {"island": lax.rem(x + d, 4) * 4 + z * 2 + c}

    at_z = {"island": x * 4 + (1 - z) * 2 + c}
    at_c = {"island": x * 4 + z * 2 + 1 - c}
    pair, link = at_y(mate), at_y(near)
    ways = (("+", at_h(1), 3), ("-", at_h(3), 1))

    r = w.shape[1]
    g = r * 4
    half = g // 2
    ca, cb = share, n - share
    A, B = pl.ds(0, ca), pl.ds(ca, cb)
    sa, sb = back_share, n - back_share
    SA, SB = pl.ds(0, sa), pl.ds(sa, sb)

    def rows(dh, at):
        return pl.ds(pl.multiple_of(dh * g + at * r, r), r)

    def group(dh):
        return pl.ds(dh * g, g)

    def low(dh):
        return pl.ds(dh * g, half)

    def high(dh):
        return pl.ds(dh * g + half, half)

    def wide(start, size):
        return pl.ds(pl.multiple_of(start, 128), size)

    def own_w(lo, size):
        return w.at[0, :, wide(base + lo, size)]

    copies = {}

    def send(name, src, dst, device):
        k = len(copies)
        copies[name] = pltpu.make_async_remote_copy(
            src_ref=src, dst_ref=dst, send_sem=ssem.at[k], recv_sem=rsem.at[k],
            device_id=device, device_id_type=MESH,
        )
        copies[name].start()

    def got(*names):
        for name in names:
            copies[name].wait_recv()

    def got_ways(*names):
        for name in names:
            got(name + "+", name + "-")

    def load(src, dst, k):
        cp = pltpu.make_async_copy(src, dst, lsem.at[k])
        cp.start()
        return cp

    cols = slab.shape[1] // groups

    def block(k):
        return wide(k * cols, cols)

    mine_rows = rows(0, y)
    lw = load(own_w(0, n), wv.at[mine_rows], 0)
    lx = load(xin.at[:, wide(base, n)], xo, 1)
    small = [load(tok, tokb, 4), load(readout, rob, 5)]
    states = [load(master, msb, 6), load(momentum, mob, 7)]
    for j in range(8):
        pltpu.make_async_copy(pg.at[0, :, block(2 * j + c)], acc.at[j], lsem.at[8]).start()

    barrier = pltpu.get_barrier_semaphore()
    partners = [pair, link, at_h(1), at_h(3), at_x(1), at_x(2), at_x(3), at_z, at_c]
    for device in partners:
        pl.semaphore_signal(barrier, inc=1, device_id=device, device_id_type=MESH)
    pl.semaphore_wait(barrier, len(partners))

    send("w", w.at[0, :, wide(mate_base, n)], wv.at[mine_rows], pair)
    for s, device, slot in ways:
        send(f"wao{s}", own_w(0, ca), wv.at[rows(slot, y), A], device)
    send("ybo", own_w(ca, cb), wv.at[mine_rows, B], link)
    for j in range(8):
        pltpu.make_async_remote_copy(
            src_ref=pg.at[0, :, block(2 * j + 1 - c)], dst_ref=rc.at[j], send_sem=gsem.at[0], recv_sem=gsem.at[1],
            device_id=at_c, device_id_type=MESH,
        ).start()

    def all_blocks(k, ref):
        return pltpu.make_async_remote_copy(
            src_ref=ref, dst_ref=ref, send_sem=gsem.at[k], recv_sem=gsem.at[k + 1], device_id=at_c, device_id_type=MESH
        )

    def product(at_rows, xs):
        def body(j, total):
            at = wide(j * (n // 4), n // 4)
            return total + lax.dot_general(
                wv[at_rows, at], xs[:, at], (((1,), (1,)), ((), ())), preferred_element_type=F32
            )

        return lax.fori_loop(0, 4, body, jnp.zeros((g, xs.shape[0]), F32))

    def pre_mate(d):
        ps[group(d)] = product(group(d), xp)
        send(f"p{d}", ps.at[group(d)], pr.at[group(d)], pair)

    def pre_own(d):
        preo[group(d)] = product(group(d), xo)

    def slope(d):
        got(f"p{d}")
        p = preo[group(d)] + pr[group(d)]
        sig = jax.nn.sigmoid(p)
        keep = (tokb[...] != 0).astype(F32)
        row = rob[pl.ds(lax.rem(h + d, 4), 1), :]
        column = jnp.transpose(jnp.broadcast_to(row, (g, g)))
        weight = jnp.concatenate([column] * (p.shape[1] // g), axis=1)
        value = scale * keep * weight * (sig * (1.0 + p * (1.0 - sig)))
        slt[group(d)] = value.astype(BF16)
        send(f"s{d}", slt.at[group(d)], spt.at[group(d)], pair)
        slo[:, group(d)] = jnp.transpose(value).astype(BF16)

    def dw(d):
        got(f"s{d}")
        own, other = slt[group(d)], spt[group(d)]

        def body(j, carry):
            at = wide(j * (n // 4), n // 4)
            part = jnp.dot(own, xo[:, at], preferred_element_type=F32) + jnp.dot(
                other, xp[:, at], preferred_element_type=F32
            )
            dwp[group(d), at] = part
            snd[group(d), at] = part.astype(BF16)
            return carry

        lax.fori_loop(0, 4, body, 0)

    def add(at_rows, lo, size, terms, to=None):
        units = size // 128
        step = 128 * max(k for k in range(1, 13 if at_rows.size == r else 6) if units % k == 0)

        def body(j, carry):
            at = wide(lo + j * step, step)
            there = wide(j * step, step)
            total = dwp[at_rows, at]
            for ref in terms:
                total = total + ref[:, there].astype(F32)
            if to != "snd":
                dwp[at_rows, at] = total
            if to != "dwp":
                snd[at_rows, at] = total.astype(BF16)
            return carry

        lax.fori_loop(0, size // step, body, 0)

    def across(d, at):
        part = wv.at[rows(d, y if at == "o" else mate), A]
        send(f"ya{d}{at}", part, part, link)

    def across_done(d):
        got(f"ya{d}o", f"ya{d}m")

    def across_back(d):
        for k, at in enumerate((near, far)):
            send(f"sa{d}{k}", snd.at[rows(d, at), SA], ra.at[d, k], link)

    def sum_across(d, to=None):
        got(f"sa{d}0", f"sa{d}1")
        add(rows(d, y), 0, sa, [ra.at[d, 0]], to)
        add(rows(d, mate), 0, sa, [ra.at[d, 1]], to)

    def dx_mate(k):
        def body(j, carry):
            at = wide(k * (n // 2) + j * (n // 4), n // 4)
            dxs[:, at] = jnp.dot(sp[...], wv[:, at], preferred_element_type=F32).astype(BF16)
            return carry

        lax.fori_loop(0, 2, body, 0)
        at = pl.ds(k * (n // 2), n // 2)
        send(f"dx{k}", dxs.at[:, at], dxb.at[:, wide(base + k * (n // 2), n // 2)], pair)

    def dx_own():
        def body(j, carry):
            at = wide(j * (n // 4), n // 4)
            there = wide(base + j * (n // 4), n // 4)
            dxb[:, there] = jnp.dot(slo[...], wv[:, at], preferred_element_type=F32).astype(BF16)
            return carry

        lax.fori_loop(0, 4, body, 0)

    got("w")
    part = wv.at[rows(0, mate), B]
    send("ybm", part, part, link)
    for s, device, slot in ways:
        send(f"wam{s}", wv.at[rows(0, mate), A], wv.at[rows(slot, mate), A], device)
    send("x", xin.at[:, wide(mate_base, n)], xp, pair)
    got("ybo", "ybm")
    lw.wait()
    for s, device, slot in ways:
        send(f"hb{s}", wv.at[group(0), B], wv.at[group(slot), B], device)
    got_ways("wao")
    send("wf+", wv.at[rows(3, y), A], wv.at[rows(2, y), A], at_h(1))
    across(3, "o")
    across(1, "o")
    got_ways("wam")
    send("wf-", wv.at[rows(1, mate), A], wv.at[rows(2, mate), A], at_h(3))
    across(3, "m")
    across(1, "m")

    pltpu.make_async_copy(acc, acc, lsem.at[8]).wait()
    all_blocks(0, rc).wait_recv()
    for j in range(8):
        acc[j] = acc[j] + rc[j]
    for d in (1, 3, 2):
        send(f"X{d}", acc.at[pl.ds(lax.rem(x + d, 4) * 2, 2)], rx.at[d - 1], at_x(d))
    got("X1", "X3", "X2")
    blocks = acc.at[pl.ds(x * 2, 2)]
    blocks[...] = blocks[...] + rx[0] + rx[1] + rx[2]

    lx.wait()
    for cp in small + states:
        cp.wait()
    got_ways("hb")
    send("hbf+", wv.at[low(3), B], wv.at[low(2), B], at_h(1))
    send("hbf-", wv.at[high(1), B], wv.at[high(2), B], at_h(3))
    send("Z", acc.at[x * 2 + 1 - z], rz, at_z)
    across_done(3)
    across_done(1)
    pre_own(3)
    got("x")
    pre_mate(3)
    pre_mate(1)
    got_ways("wf")
    pre_own(1)
    across(2, "m")
    across(2, "o")
    across(0, "m")
    slope(3)
    across(0, "o")
    slope(1)
    dw(3)
    dw(1)
    got_ways("hbf")
    send("U2+", snd.at[high(1), SB], ru0.at[0, pl.ds(half, half)], at_h(1))
    send("U2-", snd.at[low(3), SB], ru0.at[1, pl.ds(0, half)], at_h(3))
    across_done(2)
    pre_mate(2)
    pre_own(2)

    got("Z")
    mean = (acc[x * 2 + z] + rz[...]) / groups
    stepped = 0.9 * mob[...] + mean
    momentum_out[...] = stepped
    master_out[...] = msb[...] - 0.7 * (mean + 0.9 * stepped)
    mine = block(i)
    slab[:, mine] = master_out[...].astype(BF16)
    send("SZ", slab.at[:, mine], slab.at[:, mine], at_z)

    slope(2)
    across_done(0)
    pre_mate(0)
    across_back(1)
    dw(2)
    send("U1+", snd.at[low(2), SB], ru1.at[0], at_h(1))
    send("U1-", snd.at[high(2), SB], ru1.at[1], at_h(3))
    across_back(2)
    across_back(3)
    pre_own(0)
    slope(0)
    dw(0)
    across_back(0)
    sum_across(2)
    send("T1+", snd.at[rows(2, y), SA], rt1.at[0], at_h(1))
    send("T1-", snd.at[rows(2, mate), SA], rt1.at[1], at_h(3))

    got("SZ")
    other = block(x * 4 + (1 - z) * 2 + c)
    for d in (1, 3, 2):
        send(f"SX{d}", slab.at[:, mine], slab.at[:, mine], at_x(d))
        send(f"SY{d}", slab.at[:, other], slab.at[:, other], at_x(d))

    sum_across(3)
    sum_across(1)
    for d in range(4):
        sp[:, group(d)] = jnp.transpose(spt[group(d)].astype(F32)).astype(BF16)
    dx_mate(1)
    got_ways("U1")
    add(low(1), sa, sb, [ru1.at[0]], "snd")
    add(high(3), sa, sb, [ru1.at[1]], "snd")
    send("U3+", snd.at[low(1), SB], ru0.at[0, pl.ds(0, half)], at_h(1))
    send("U3-", snd.at[high(3), SB], ru0.at[1, pl.ds(half, half)], at_h(3))
    dx_mate(0)
    got_ways("T1")
    add(rows(1, y), 0, sa, [rt1.at[0]], "snd")
    add(rows(3, mate), 0, sa, [rt1.at[1]], "snd")
    send("T3+", snd.at[rows(1, y), SA], rt0.at[0, 0], at_h(1))
    send("T3-", snd.at[rows(3, mate), SA], rt0.at[1, 1], at_h(3))
    send("T2+", snd.at[rows(1, mate), SA], rt0.at[0, 1], at_h(1))
    send("T2-", snd.at[rows(3, y), SA], rt0.at[1, 0], at_h(3))
    sum_across(0, "dwp")
    dx_own()

    got("SX1", "SX3", "SX2", "SY1", "SY3", "SY2")
    for j in range(8):
        at = block(2 * j + c)
        pltpu.make_async_remote_copy(
            src_ref=slab.at[:, at], dst_ref=slab.at[:, at], send_sem=gsem.at[2], recv_sem=gsem.at[3],
            device_id=at_c, device_id_type=MESH,
        ).start()

    got_ways("U2", "U3")
    add(group(0), sa, sb, [ru0.at[0], ru0.at[1]])
    for k, at in enumerate((near, far)):
        send(f"sb{k}", snd.at[rows(0, at), SB], rb.at[k], link)
    got("sb0", "sb1")
    add(rows(0, mate), sa, sb, [rb.at[1]], "snd")
    send("fb", snd.at[rows(0, mate), SB], rs.at[:, SB], pair)
    add(mine_rows, sa, sb, [rb.at[0]], "dwp")
    got_ways("T2", "T3")
    add(rows(0, mate), 0, sa, [rt0.at[0, 1], rt0.at[1, 1]], "snd")
    send("fa", snd.at[rows(0, mate), SA], rs.at[:, SA], pair)
    add(mine_rows, 0, sa, [rt0.at[0, 0], rt0.at[1, 0]], "dwp")
    wg_out[0, :, wide(base, n)] = dwp[mine_rows, :]
    got("fa", "fb")
    wg_out[0, :, wide(mate_base, n)] = rs[...].astype(F32)
    got("dx0", "dx1")
    all_blocks(2, slab.at[:, pl.ds(0, slab.shape[1] // 2)]).wait_recv()

    for copy in copies.values():
        copy.wait_send()
    all_blocks(0, rc).wait_send()
    all_blocks(2, slab.at[:, pl.ds(0, slab.shape[1] // 2)]).wait_send()


def drain(*refs):
    sems = refs[-1]
    moves = [pltpu.make_async_copy(refs[n], refs[5 + n], sems.at[n]) for n in range(5)]
    for move in moves:
        move.start()
    for move in moves:
        move.wait()


def on_device(pseudo_grads, master_slab, momentum, inner_inputs, token_ids, inner_weight, readout):
    groups = lax.axis_size("island")
    tokens, k = inner_inputs.shape
    r = inner_weight.shape[1]
    features = readout.shape[0]
    g = 4 * r
    width, cols = pseudo_grads.shape[2], master_slab.shape[1]
    out_rows = pseudo_grads.shape[1]
    n = k // 2
    share, back_share = 10 * n // 16, 10 * n // 16
    sa, sb = back_share, n - back_share
    scale = 1.0 / math.sqrt(tokens * lax.axis_size("fsdp"))
    V, sem = pltpu.VMEM, pltpu.SemaphoreType.DMA
    anywhere = pl.BlockSpec(memory_space=pl.ANY)

    def body(*refs):
        kernel(groups, share, back_share, scale, *refs)

    shapes = (
        ((out_rows, width), BF16),
        (master_slab.shape, F32),
        (momentum.shape, F32),
        ((1, r, k), F32),
        ((tokens, k), BF16),
    )
    results = pl.pallas_call(
        body,
        out_shape=tuple(V(*shape) for shape in shapes),
        in_specs=[anywhere] * 7,
        out_specs=[pl.BlockSpec(memory_space=pltpu.VMEM)] * 5,
        scratch_shapes=[
            V((tokens, n), BF16),
            V((tokens, n), BF16),
            V((features, n), BF16),
            V((features, n), F32),
            V((features, n), BF16),
            V((features, tokens), BF16),
            V((tokens, features), BF16),
            V((features, tokens), BF16),
            V((tokens, features), BF16),
            V((tokens, n), BF16),
            V((1, tokens), jnp.int32),
            V((4, g), F32),
            V((features, tokens), F32),
            V((features, tokens), F32),
            V((features, tokens), F32),
            V((4, 2, r, sa), BF16),
            V((2, r, sa), BF16),
            V((2, 2, r, sa), BF16),
            V((2, g // 2, sb), BF16),
            V((2, g, sb), BF16),
            V((2, r, sb), BF16),
            V((r, n), BF16),
            V((8, out_rows, cols), F32),
            V((8, out_rows, cols), F32),
            V((3, 2, out_rows, cols), F32),
            V((out_rows, cols), F32),
            V((out_rows, cols), F32),
            V((out_rows, cols), F32),
            sem((N_SEMS,)),
            sem((N_SEMS,)),
            sem((12,)),
            sem((4,)),
        ],
        compiler_params=pltpu.CompilerParams(
            collective_id=0, has_side_effects=True, vmem_limit_bytes=54 * 2**20
        ),
        name="window",
    )(
        pseudo_grads, master_slab, momentum, inner_inputs, token_ids.reshape(1, tokens),
        inner_weight, readout.reshape(4, g),
    )
    return pl.pallas_call(
        drain,
        out_shape=tuple(jax.ShapeDtypeStruct(*shape) for shape in shapes),
        in_specs=[pl.BlockSpec(memory_space=pltpu.VMEM)] * 5,
        out_specs=[anywhere] * 5,
        scratch_shapes=[sem((5,))],
        compiler_params=pltpu.CompilerParams(vmem_limit_bytes=2**20),
        name="drain",
    )(*(pltpu.with_memory_space_constraint(result, pltpu.VMEM) for result in results))


def solution(mesh):
    in_specs = (
        P("island", "fsdp", None),
        P("fsdp", "island"),
        P("fsdp", "island"),
        P(("island", "fsdp"), None),
        P(("island", "fsdp")),
        P("island", "fsdp", None),
        P(),
    )
    out_specs = (
        P("fsdp", None),
        P("fsdp", "island"),
        P("fsdp", "island"),
        P("island", "fsdp", None),
        P(("island", "fsdp"), None),
    )
    return jax.shard_map(
        on_device, mesh=mesh, in_specs=in_specs, out_specs=out_specs, check_vma=False
    )
```

```python
import math

import jax
import jax.numpy as jnp
from jax import lax
from jax.experimental import pallas as pl
from jax.experimental.pallas import tpu as pltpu
from jax.sharding import PartitionSpec as P

MESH = pl.DeviceIdType.MESH
F32, BF16 = jnp.float32, jnp.bfloat16
N_SEMS = 96


def kernel(
    groups, share, back_share, scale,
    pg, master, momentum, xin, tok, w, readout,
    slab, master_out, momentum_out, wg_out, dxb,
    xo, xp, wv, dwp, snd, slt, slo, spt, sp, dxs, tokb, rob, preo, ps, pr,
    ra, rt1, rt0, ru1, ru0, rb, rs,
    acc, rc, rx, rz, msb, mob,
    ssem, rsem, lsem, gsem,
):
    f, i = lax.axis_index("fsdp"), lax.axis_index("island")
    h, y = f // 4, lax.rem(f, 4)
    x, z, c = i // 4, lax.rem(i // 2, 2), lax.rem(i, 2)

    one, two = y + 1 - 2 * lax.rem(y, 2), 3 - y
    mate = one + c * (two - one)
    near = two + c * (one - two)
    far = 3 - one
    n = xo.shape[1]
    side = lax.rem((y + 1) // 2, 2) * (1 - c) + (y // 2) * c
    base, mate_base = n * side, n * (1 - side)

    def at_y(d):
        return {"fsdp": h * 4 + d}

    def at_h(d):
        return {"fsdp": lax.rem(h + d, 4) * 4 + y}

    def at_x(d):
        return {"island": lax.rem(x + d, 4) * 4 + z * 2 + c}

    at_z = {"island": x * 4 + (1 - z) * 2 + c}
    at_c = {"island": x * 4 + z * 2 + 1 - c}
    pair, link = at_y(mate), at_y(near)
    ways = (("+", at_h(1), 3), ("-", at_h(3), 1))

    r = w.shape[1]
    g = r * 4
    half = g // 2
    ca, cb = share, n - share
    A, B = pl.ds(0, ca), pl.ds(ca, cb)
    sa, sb = back_share, n - back_share
    SA, SB = pl.ds(0, sa), pl.ds(sa, sb)

    def rows(dh, at):
        return pl.ds(pl.multiple_of(dh * g + at * r, r), r)

    def group(dh):
        return pl.ds(dh * g, g)

    def low(dh):
        return pl.ds(dh * g, half)

    def high(dh):
        return pl.ds(dh * g + half, half)

    def wide(start, size):
        return pl.ds(pl.multiple_of(start, 128), size)

    def own_w(lo, size):
        return w.at[0, :, wide(base + lo, size)]

    copies = {}

    def send(name, src, dst, device):
        k = len(copies)
        copies[name] = pltpu.make_async_remote_copy(
            src_ref=src, dst_ref=dst, send_sem=ssem.at[k], recv_sem=rsem.at[k],
            device_id=device, device_id_type=MESH,
        )
        copies[name].start()

    def got(*names):
        for name in names:
            copies[name].wait_recv()

    def got_ways(*names):
        for name in names:
            got(name + "+", name + "-")

    def load(src, dst, k):
        cp = pltpu.make_async_copy(src, dst, lsem.at[k])
        cp.start()
        return cp

    cols = slab.shape[1] // groups

    def block(k):
        return wide(k * cols, cols)

    mine_rows = rows(0, y)
    lw = load(own_w(0, n), wv.at[mine_rows], 0)
    lx = load(xin.at[:, wide(base, n)], xo, 1)
    small = [load(tok, tokb, 4), load(readout, rob, 5)]
    states = [load(master, msb, 6), load(momentum, mob, 7)]
    for j in range(8):
        pltpu.make_async_copy(pg.at[0, :, block(2 * j + c)], acc.at[j], lsem.at[8]).start()

    barrier = pltpu.get_barrier_semaphore()
    partners = [pair, link, at_h(1), at_h(3), at_x(1), at_x(2), at_x(3), at_z, at_c]
    for device in partners:
        pl.semaphore_signal(barrier, inc=1, device_id=device, device_id_type=MESH)
    pl.semaphore_wait(barrier, len(partners))

    send("w", w.at[0, :, wide(mate_base, n)], wv.at[mine_rows], pair)
    for s, device, slot in ways:
        send(f"wao{s}", own_w(0, ca), wv.at[rows(slot, y), A], device)
    send("ybo", own_w(ca, cb), wv.at[mine_rows, B], link)
    for j in range(8):
        pltpu.make_async_remote_copy(
            src_ref=pg.at[0, :, block(2 * j + 1 - c)], dst_ref=rc.at[j], send_sem=gsem.at[0], recv_sem=gsem.at[1],
            device_id=at_c, device_id_type=MESH,
        ).start()

    def all_blocks(k, ref):
        return pltpu.make_async_remote_copy(
            src_ref=ref, dst_ref=ref, send_sem=gsem.at[k], recv_sem=gsem.at[k + 1], device_id=at_c, device_id_type=MESH
        )

    def product(at_rows, xs):
        def body(j, total):
            at = wide(j * (n // 4), n // 4)
            return total + lax.dot_general(
                wv[at_rows, at], xs[:, at], (((1,), (1,)), ((), ())), preferred_element_type=F32
            )

        return lax.fori_loop(0, 4, body, jnp.zeros((g, xs.shape[0]), F32))

    def pre_mate(d):
        ps[group(d)] = product(group(d), xp)
        send(f"p{d}", ps.at[group(d)], pr.at[group(d)], pair)

    def pre_own(d):
        preo[group(d)] = product(group(d), xo)

    def slope(d):
        got(f"p{d}")
        p = preo[group(d)] + pr[group(d)]
        sig = jax.nn.sigmoid(p)
        keep = (tokb[...] != 0).astype(F32)
        row = rob[pl.ds(lax.rem(h + d, 4), 1), :]
        column = jnp.transpose(jnp.broadcast_to(row, (g, g)))
        weight = jnp.concatenate([column] * (p.shape[1] // g), axis=1)
        value = scale * keep * weight * (sig * (1.0 + p * (1.0 - sig)))
        slt[group(d)] = value.astype(BF16)
        send(f"s{d}", slt.at[group(d)], spt.at[group(d)], pair)
        slo[:, group(d)] = jnp.transpose(value).astype(BF16)

    def dw(d):
        got(f"s{d}")
        own, other = slt[group(d)], spt[group(d)]

        def body(j, carry):
            at = wide(j * (n // 4), n // 4)
            part = jnp.dot(own, xo[:, at], preferred_element_type=F32) + jnp.dot(
                other, xp[:, at], preferred_element_type=F32
            )
            dwp[group(d), at] = part
            snd[group(d), at] = part.astype(BF16)
            return carry

        lax.fori_loop(0, 4, body, 0)

    def add(at_rows, lo, size, terms, to=None):
        units = size // 128
        step = 128 * max(k for k in range(1, 13 if at_rows.size == r else 6) if units % k == 0)

        def body(j, carry):
            at = wide(lo + j * step, step)
            there = wide(j * step, step)
            total = dwp[at_rows, at]
            for ref in terms:
                total = total + ref[:, there].astype(F32)
            if to != "snd":
                dwp[at_rows, at] = total
            if to != "dwp":
                snd[at_rows, at] = total.astype(BF16)
            return carry

        lax.fori_loop(0, size // step, body, 0)

    def across(d, at):
        part = wv.at[rows(d, y if at == "o" else mate), A]
        send(f"ya{d}{at}", part, part, link)

    def across_done(d):
        got(f"ya{d}o", f"ya{d}m")

    def across_back(d):
        for k, at in enumerate((near, far)):
            send(f"sa{d}{k}", snd.at[rows(d, at), SA], ra.at[d, k], link)

    def sum_across(d, to=None):
        got(f"sa{d}0", f"sa{d}1")
        add(rows(d, y), 0, sa, [ra.at[d, 0]], to)
        add(rows(d, mate), 0, sa, [ra.at[d, 1]], to)

    def dx_mate(k):
        def body(j, carry):
            at = wide(k * (n // 2) + j * (n // 4), n // 4)
            dxs[:, at] = jnp.dot(sp[...], wv[:, at], preferred_element_type=F32).astype(BF16)
            return carry

        lax.fori_loop(0, 2, body, 0)
        at = pl.ds(k * (n // 2), n // 2)
        send(f"dx{k}", dxs.at[:, at], dxb.at[:, wide(base + k * (n // 2), n // 2)], pair)

    def dx_own():
        def body(j, carry):
            at = wide(j * (n // 4), n // 4)
            there = wide(base + j * (n // 4), n // 4)
            dxb[:, there] = jnp.dot(slo[...], wv[:, at], preferred_element_type=F32).astype(BF16)
            return carry

        lax.fori_loop(0, 4, body, 0)

    got("w")
    part = wv.at[rows(0, mate), B]
    send("ybm", part, part, link)
    for s, device, slot in ways:
        send(f"wam{s}", wv.at[rows(0, mate), A], wv.at[rows(slot, mate), A], device)
    send("x", xin.at[:, wide(mate_base, n)], xp, pair)
    got("ybo", "ybm")
    lw.wait()
    for s, device, slot in ways:
        send(f"hb{s}", wv.at[group(0), B], wv.at[group(slot), B], device)
    got_ways("wao")
    send("wf+", wv.at[rows(3, y), A], wv.at[rows(2, y), A], at_h(1))
    across(3, "o")
    across(1, "o")
    got_ways("wam")
    send("wf-", wv.at[rows(1, mate), A], wv.at[rows(2, mate), A], at_h(3))
    across(3, "m")
    across(1, "m")

    pltpu.make_async_copy(acc, acc, lsem.at[8]).wait()
    all_blocks(0, rc).wait_recv()
    for j in range(8):
        acc[j] = acc[j] + rc[j]
    for d in (1, 3, 2):
        send(f"X{d}", acc.at[pl.ds(lax.rem(x + d, 4) * 2, 2)], rx.at[d - 1], at_x(d))
    got("X1", "X3", "X2")
    blocks = acc.at[pl.ds(x * 2, 2)]
    blocks[...] = blocks[...] + rx[0] + rx[1] + rx[2]

    lx.wait()
    for cp in small + states:
        cp.wait()
    got_ways("hb")
    send("hbf+", wv.at[low(3), B], wv.at[low(2), B], at_h(1))
    send("hbf-", wv.at[high(1), B], wv.at[high(2), B], at_h(3))
    send("Z", acc.at[x * 2 + 1 - z], rz, at_z)
    across_done(3)
    across_done(1)
    pre_own(3)
    got("x")
    pre_mate(3)
    pre_mate(1)
    got_ways("wf")
    pre_own(1)
    across(2, "m")
    across(2, "o")
    across(0, "m")
    slope(3)
    across(0, "o")
    slope(1)
    dw(3)
    dw(1)
    got_ways("hbf")
    send("U2+", snd.at[high(1), SB], ru0.at[0, pl.ds(half, half)], at_h(1))
    send("U2-", snd.at[low(3), SB], ru0.at[1, pl.ds(0, half)], at_h(3))
    across_done(2)
    pre_mate(2)
    pre_own(2)

    got("Z")
    mean = (acc[x * 2 + z] + rz[...]) / groups
    stepped = 0.9 * mob[...] + mean
    momentum_out[...] = stepped
    master_out[...] = msb[...] - 0.7 * (mean + 0.9 * stepped)
    mine = block(i)
    slab[:, mine] = master_out[...].astype(BF16)
    send("SZ", slab.at[:, mine], slab.at[:, mine], at_z)

    slope(2)
    across_done(0)
    pre_mate(0)
    across_back(1)
    dw(2)
    send("U1+", snd.at[low(2), SB], ru1.at[0], at_h(1))
    send("U1-", snd.at[high(2), SB], ru1.at[1], at_h(3))
    across_back(2)
    across_back(3)
    pre_own(0)
    slope(0)
    dw(0)
    across_back(0)
    sum_across(2)
    send("T1+", snd.at[rows(2, y), SA], rt1.at[0], at_h(1))
    send("T1-", snd.at[rows(2, mate), SA], rt1.at[1], at_h(3))

    got("SZ")
    other = block(x * 4 + (1 - z) * 2 + c)
    for d in (1, 3, 2):
        send(f"SX{d}", slab.at[:, mine], slab.at[:, mine], at_x(d))
        send(f"SY{d}", slab.at[:, other], slab.at[:, other], at_x(d))

    sum_across(3)
    sum_across(1)
    for d in range(4):
        sp[:, group(d)] = jnp.transpose(spt[group(d)].astype(F32)).astype(BF16)
    dx_mate(1)
    got_ways("U1")
    add(low(1), sa, sb, [ru1.at[0]], "snd")
    add(high(3), sa, sb, [ru1.at[1]], "snd")
    send("U3+", snd.at[low(1), SB], ru0.at[0, pl.ds(0, half)], at_h(1))
    send("U3-", snd.at[high(3), SB], ru0.at[1, pl.ds(half, half)], at_h(3))
    send("T2+", snd.at[rows(1, mate), SA], rt0.at[0, 1], at_h(1))
    dx_mate(0)
    got_ways("T1")
    add(rows(3, mate), 0, sa, [rt1.at[1]], "snd")
    send("T3-", snd.at[rows(3, mate), SA], rt0.at[1, 1], at_h(3))
    send("T2-", snd.at[rows(3, y), SA], rt0.at[1, 0], at_h(3))
    add(rows(1, y), 0, sa, [rt1.at[0]], "snd")
    send("T3+", snd.at[rows(1, y), SA], rt0.at[0, 0], at_h(1))
    sum_across(0, "dwp")
    dx_own()

    got("SX1", "SX3", "SX2", "SY1", "SY3", "SY2")
    for j in range(8):
        at = block(2 * j + c)
        pltpu.make_async_remote_copy(
            src_ref=slab.at[:, at], dst_ref=slab.at[:, at], send_sem=gsem.at[2], recv_sem=gsem.at[3],
            device_id=at_c, device_id_type=MESH,
        ).start()

    got_ways("U2", "U3")
    add(group(0), sa, sb, [ru0.at[0], ru0.at[1]])
    for k, at in enumerate((near, far)):
        send(f"sb{k}", snd.at[rows(0, at), SB], rb.at[k], link)
    got("T2+", "T3-")
    add(rows(0, mate), 0, sa, [rt0.at[0, 1], rt0.at[1, 1]], "snd")
    send("fa", snd.at[rows(0, mate), SA], rs.at[:, SA], pair)
    got("sb0", "sb1")
    add(rows(0, mate), sa, sb, [rb.at[1]], "snd")
    send("fb", snd.at[rows(0, mate), SB], rs.at[:, SB], pair)
    add(mine_rows, sa, sb, [rb.at[0]], "dwp")
    wg_out[0, :, wide(base + sa, sb)] = dwp[mine_rows, SB]
    got("fa", "fb")
    wg_out[0, :, wide(mate_base, n)] = rs[...].astype(F32)
    got("dx0", "dx1")
    all_blocks(2, slab.at[:, pl.ds(0, slab.shape[1] // 2)]).wait_recv()
    got("T3+", "T2-")
    wg_out[0, :, wide(base, sa)] = dwp[mine_rows, SA] + rt0[0, 0].astype(F32) + rt0[1, 0].astype(F32)

    for copy in copies.values():
        copy.wait_send()
    all_blocks(0, rc).wait_send()
    all_blocks(2, slab.at[:, pl.ds(0, slab.shape[1] // 2)]).wait_send()


def drain(*refs):
    sems = refs[-1]
    moves = [pltpu.make_async_copy(refs[n], refs[5 + n], sems.at[n]) for n in range(5)]
    for move in moves:
        move.start()
    for move in moves:
        move.wait()


def on_device(pseudo_grads, master_slab, momentum, inner_inputs, token_ids, inner_weight, readout):
    groups = lax.axis_size("island")
    tokens, k = inner_inputs.shape
    r = inner_weight.shape[1]
    features = readout.shape[0]
    g = 4 * r
    width, cols = pseudo_grads.shape[2], master_slab.shape[1]
    out_rows = pseudo_grads.shape[1]
    n = k // 2
    share, back_share = 10 * n // 16, 10 * n // 16
    sa, sb = back_share, n - back_share
    scale = 1.0 / math.sqrt(tokens * lax.axis_size("fsdp"))
    V, sem = pltpu.VMEM, pltpu.SemaphoreType.DMA
    anywhere = pl.BlockSpec(memory_space=pl.ANY)

    def body(*refs):
        kernel(groups, share, back_share, scale, *refs)

    shapes = (
        ((out_rows, width), BF16),
        (master_slab.shape, F32),
        (momentum.shape, F32),
        ((1, r, k), F32),
        ((tokens, k), BF16),
    )
    results = pl.pallas_call(
        body,
        out_shape=tuple(V(*shape) for shape in shapes),
        in_specs=[anywhere] * 7,
        out_specs=[pl.BlockSpec(memory_space=pltpu.VMEM)] * 5,
        scratch_shapes=[
            V((tokens, n), BF16),
            V((tokens, n), BF16),
            V((features, n), BF16),
            V((features, n), F32),
            V((features, n), BF16),
            V((features, tokens), BF16),
            V((tokens, features), BF16),
            V((features, tokens), BF16),
            V((tokens, features), BF16),
            V((tokens, n), BF16),
            V((1, tokens), jnp.int32),
            V((4, g), F32),
            V((features, tokens), F32),
            V((features, tokens), F32),
            V((features, tokens), F32),
            V((4, 2, r, sa), BF16),
            V((2, r, sa), BF16),
            V((2, 2, r, sa), BF16),
            V((2, g // 2, sb), BF16),
            V((2, g, sb), BF16),
            V((2, r, sb), BF16),
            V((r, n), BF16),
            V((8, out_rows, cols), F32),
            V((8, out_rows, cols), F32),
            V((3, 2, out_rows, cols), F32),
            V((out_rows, cols), F32),
            V((out_rows, cols), F32),
            V((out_rows, cols), F32),
            sem((N_SEMS,)),
            sem((N_SEMS,)),
            sem((12,)),
            sem((4,)),
        ],
        compiler_params=pltpu.CompilerParams(
            collective_id=0, has_side_effects=True, vmem_limit_bytes=54 * 2**20
        ),
        name="window",
    )(
        pseudo_grads, master_slab, momentum, inner_inputs, token_ids.reshape(1, tokens),
        inner_weight, readout.reshape(4, g),
    )
    return pl.pallas_call(
        drain,
        out_shape=tuple(jax.ShapeDtypeStruct(*shape) for shape in shapes),
        in_specs=[pl.BlockSpec(memory_space=pltpu.VMEM)] * 5,
        out_specs=[anywhere] * 5,
        scratch_shapes=[sem((5,))],
        compiler_params=pltpu.CompilerParams(vmem_limit_bytes=2**20),
        name="drain",
    )(*(pltpu.with_memory_space_constraint(result, pltpu.VMEM) for result in results))


def solution(mesh):
    in_specs = (
        P("island", "fsdp", None),
        P("fsdp", "island"),
        P("fsdp", "island"),
        P(("island", "fsdp"), None),
        P(("island", "fsdp")),
        P("island", "fsdp", None),
        P(),
    )
    out_specs = (
        P("fsdp", None),
        P("fsdp", "island"),
        P("fsdp", "island"),
        P("island", "fsdp", None),
        P(("island", "fsdp"), None),
    )
    return jax.shard_map(
        on_device, mesh=mesh, in_specs=in_specs, out_specs=out_specs, check_vma=False
    )
```

```python
import math

import jax
import jax.numpy as jnp
from jax import lax
from jax.experimental import pallas as pl
from jax.experimental.pallas import tpu as pltpu
from jax.sharding import PartitionSpec as P

MESH = pl.DeviceIdType.MESH
F32, BF16 = jnp.float32, jnp.bfloat16
N_SEMS = 96


def kernel(
    groups, share, back_share, scale,
    pg, master, momentum, xin, tok, w, readout,
    slab, master_out, momentum_out, wg_out, dxb,
    xo, xp, wv, dwp, snd, slt, slo, spt, sp, dxs, tokb, rob, preo, ps, pr,
    ra, rt1, rt0, ru1, ru0, rb, rs,
    acc, rc, rx, rz, msb, mob,
    ssem, rsem, lsem, gsem,
):
    f, i = lax.axis_index("fsdp"), lax.axis_index("island")
    h, y = f // 4, lax.rem(f, 4)
    x, z, c = i // 4, lax.rem(i // 2, 2), lax.rem(i, 2)

    one, two = y + 1 - 2 * lax.rem(y, 2), 3 - y
    mate = one + c * (two - one)
    near = two + c * (one - two)
    far = 3 - one
    n = xo.shape[1]
    side = lax.rem((y + 1) // 2, 2) * (1 - c) + (y // 2) * c
    base, mate_base = n * side, n * (1 - side)

    def at_y(d):
        return {"fsdp": h * 4 + d}

    def at_h(d):
        return {"fsdp": lax.rem(h + d, 4) * 4 + y}

    def at_x(d):
        return {"island": lax.rem(x + d, 4) * 4 + z * 2 + c}

    at_z = {"island": x * 4 + (1 - z) * 2 + c}
    at_c = {"island": x * 4 + z * 2 + 1 - c}
    pair, link = at_y(mate), at_y(near)
    ways = (("+", at_h(1), 3), ("-", at_h(3), 1))

    r = w.shape[1]
    g = r * 4
    half = g // 2
    ca, cb = share, n - share
    A, B = pl.ds(0, ca), pl.ds(ca, cb)
    sa, sb = back_share, n - back_share
    SA, SB = pl.ds(0, sa), pl.ds(sa, sb)

    def rows(dh, at):
        return pl.ds(pl.multiple_of(dh * g + at * r, r), r)

    def group(dh):
        return pl.ds(dh * g, g)

    def low(dh):
        return pl.ds(dh * g, half)

    def high(dh):
        return pl.ds(dh * g + half, half)

    def wide(start, size):
        return pl.ds(pl.multiple_of(start, 128), size)

    def own_w(lo, size):
        return w.at[0, :, wide(base + lo, size)]

    copies = {}

    def send(name, src, dst, device):
        k = len(copies)
        copies[name] = pltpu.make_async_remote_copy(
            src_ref=src, dst_ref=dst, send_sem=ssem.at[k], recv_sem=rsem.at[k],
            device_id=device, device_id_type=MESH,
        )
        copies[name].start()

    def got(*names):
        for name in names:
            copies[name].wait_recv()

    def got_ways(*names):
        for name in names:
            got(name + "+", name + "-")

    def load(src, dst, k):
        cp = pltpu.make_async_copy(src, dst, lsem.at[k])
        cp.start()
        return cp

    cols = slab.shape[1] // groups

    def block(k):
        return wide(k * cols, cols)

    mine_rows = rows(0, y)
    lw = load(own_w(0, n), wv.at[mine_rows], 0)
    lx = load(xin.at[:, wide(base, n)], xo, 1)
    small = [load(tok, tokb, 4), load(readout, rob, 5)]
    states = [load(master, msb, 6), load(momentum, mob, 7)]
    for j in range(8):
        pltpu.make_async_copy(pg.at[0, :, block(2 * j + c)], acc.at[j], lsem.at[8]).start()

    barrier = pltpu.get_barrier_semaphore()
    partners = [pair, link, at_h(1), at_h(3), at_x(1), at_x(2), at_x(3), at_z, at_c]
    for device in partners:
        pl.semaphore_signal(barrier, inc=1, device_id=device, device_id_type=MESH)
    pl.semaphore_wait(barrier, len(partners))

    send("w", w.at[0, :, wide(mate_base, n)], wv.at[mine_rows], pair)
    for s, device, slot in ways:
        send(f"wao{s}", own_w(0, ca), wv.at[rows(slot, y), A], device)
    send("ybo", own_w(ca, cb), wv.at[mine_rows, B], link)
    for j in range(8):
        pltpu.make_async_remote_copy(
            src_ref=pg.at[0, :, block(2 * j + 1 - c)], dst_ref=rc.at[j], send_sem=gsem.at[0], recv_sem=gsem.at[1],
            device_id=at_c, device_id_type=MESH,
        ).start()

    def all_blocks(k, ref):
        return pltpu.make_async_remote_copy(
            src_ref=ref, dst_ref=ref, send_sem=gsem.at[k], recv_sem=gsem.at[k + 1], device_id=at_c, device_id_type=MESH
        )

    def product(at_rows, xs):
        def body(j, total):
            at = wide(j * (n // 4), n // 4)
            return total + lax.dot_general(
                wv[at_rows, at], xs[:, at], (((1,), (1,)), ((), ())), preferred_element_type=F32
            )

        return lax.fori_loop(0, 4, body, jnp.zeros((g, xs.shape[0]), F32))

    def pre_mate(d):
        ps[group(d)] = product(group(d), xp)
        send(f"p{d}", ps.at[group(d)], pr.at[group(d)], pair)

    def pre_own(d):
        preo[group(d)] = product(group(d), xo)

    def slope(d):
        got(f"p{d}")
        p = preo[group(d)] + pr[group(d)]
        sig = jax.nn.sigmoid(p)
        keep = (tokb[...] != 0).astype(F32)
        row = rob[pl.ds(lax.rem(h + d, 4), 1), :]
        column = jnp.transpose(jnp.broadcast_to(row, (g, g)))
        weight = jnp.concatenate([column] * (p.shape[1] // g), axis=1)
        value = scale * keep * weight * (sig * (1.0 + p * (1.0 - sig)))
        slt[group(d)] = value.astype(BF16)
        send(f"s{d}", slt.at[group(d)], spt.at[group(d)], pair)
        slo[:, group(d)] = jnp.transpose(value).astype(BF16)

    def dw(d):
        got(f"s{d}")
        own, other = slt[group(d)], spt[group(d)]

        def body(j, carry):
            at = wide(j * (n // 4), n // 4)
            part = jnp.dot(own, xo[:, at], preferred_element_type=F32) + jnp.dot(
                other, xp[:, at], preferred_element_type=F32
            )
            dwp[group(d), at] = part
            snd[group(d), at] = part.astype(BF16)
            return carry

        lax.fori_loop(0, 4, body, 0)

    def add(at_rows, lo, size, terms, to=None):
        units = size // 128
        step = 128 * max(k for k in range(1, 13 if at_rows.size == r else 6) if units % k == 0)

        def body(j, carry):
            at = wide(lo + j * step, step)
            there = wide(j * step, step)
            total = dwp[at_rows, at]
            for ref in terms:
                total = total + ref[:, there].astype(F32)
            if to != "snd":
                dwp[at_rows, at] = total
            if to != "dwp":
                snd[at_rows, at] = total.astype(BF16)
            return carry

        lax.fori_loop(0, size // step, body, 0)

    def across(d, at):
        part = wv.at[rows(d, y if at == "o" else mate), A]
        send(f"ya{d}{at}", part, part, link)

    def across_done(d):
        got(f"ya{d}o", f"ya{d}m")

    def across_back(d):
        for k, at in enumerate((near, far)):
            send(f"sa{d}{k}", snd.at[rows(d, at), SA], ra.at[d, k], link)

    def sum_across(d, to=None):
        got(f"sa{d}0", f"sa{d}1")
        add(rows(d, y), 0, sa, [ra.at[d, 0]], to)
        add(rows(d, mate), 0, sa, [ra.at[d, 1]], to)

    def dx_mate(k):
        def body(j, carry):
            at = wide(k * (n // 2) + j * (n // 4), n // 4)
            dxs[:, at] = jnp.dot(sp[...], wv[:, at], preferred_element_type=F32).astype(BF16)
            return carry

        lax.fori_loop(0, 2, body, 0)
        at = pl.ds(k * (n // 2), n // 2)
        send(f"dx{k}", dxs.at[:, at], dxb.at[:, wide(base + k * (n // 2), n // 2)], pair)

    def dx_own():
        def body(j, carry):
            at = wide(j * (n // 4), n // 4)
            there = wide(base + j * (n // 4), n // 4)
            dxb[:, there] = jnp.dot(slo[...], wv[:, at], preferred_element_type=F32).astype(BF16)
            return carry

        lax.fori_loop(0, 4, body, 0)

    got("w")
    part = wv.at[rows(0, mate), B]
    send("ybm", part, part, link)
    for s, device, slot in ways:
        send(f"wam{s}", wv.at[rows(0, mate), A], wv.at[rows(slot, mate), A], device)
    send("x", xin.at[:, wide(mate_base, n)], xp, pair)
    got("ybo", "ybm")
    lw.wait()
    for s, device, slot in ways:
        send(f"hb{s}", wv.at[group(0), B], wv.at[group(slot), B], device)
    got_ways("wao")
    send("wf+", wv.at[rows(3, y), A], wv.at[rows(2, y), A], at_h(1))
    across(3, "o")
    across(1, "o")
    got_ways("wam")
    send("wf-", wv.at[rows(1, mate), A], wv.at[rows(2, mate), A], at_h(3))
    across(3, "m")
    across(1, "m")

    pltpu.make_async_copy(acc, acc, lsem.at[8]).wait()
    all_blocks(0, rc).wait_recv()
    for j in range(8):
        acc[j] = acc[j] + rc[j]
    for d in (1, 3, 2):
        send(f"X{d}", acc.at[pl.ds(lax.rem(x + d, 4) * 2, 2)], rx.at[d - 1], at_x(d))
    got("X1", "X3", "X2")
    blocks = acc.at[pl.ds(x * 2, 2)]
    blocks[...] = blocks[...] + rx[0] + rx[1] + rx[2]

    lx.wait()
    for cp in small + states:
        cp.wait()
    got_ways("hb")
    send("hbf+", wv.at[low(3), B], wv.at[low(2), B], at_h(1))
    send("hbf-", wv.at[high(1), B], wv.at[high(2), B], at_h(3))
    send("Z", acc.at[x * 2 + 1 - z], rz, at_z)
    across_done(3)
    across_done(1)
    pre_own(3)
    got("x")
    pre_mate(3)
    pre_mate(1)
    got_ways("wf")
    pre_own(1)
    across(2, "m")
    across(2, "o")
    across(0, "m")
    slope(3)
    across(0, "o")
    slope(1)
    dw(3)
    send("U2-", snd.at[low(3), SB], ru0.at[1, pl.ds(0, half)], at_h(3))
    got_ways("hbf")
    across_done(2)
    pre_mate(2)
    dw(1)
    send("U2+", snd.at[high(1), SB], ru0.at[0, pl.ds(half, half)], at_h(1))
    pre_own(2)

    got("Z")
    mean = (acc[x * 2 + z] + rz[...]) / groups
    stepped = 0.9 * mob[...] + mean
    momentum_out[...] = stepped
    master_out[...] = msb[...] - 0.7 * (mean + 0.9 * stepped)
    mine = block(i)
    slab[:, mine] = master_out[...].astype(BF16)
    send("SZ", slab.at[:, mine], slab.at[:, mine], at_z)

    slope(2)
    across_done(0)
    pre_mate(0)
    across_back(1)
    dw(2)
    send("U1+", snd.at[low(2), SB], ru1.at[0], at_h(1))
    send("U1-", snd.at[high(2), SB], ru1.at[1], at_h(3))
    across_back(2)
    across_back(3)
    pre_own(0)
    slope(0)
    dw(0)
    across_back(0)
    sum_across(2)
    send("T1+", snd.at[rows(2, y), SA], rt1.at[0], at_h(1))
    send("T1-", snd.at[rows(2, mate), SA], rt1.at[1], at_h(3))

    got("SZ")
    other = block(x * 4 + (1 - z) * 2 + c)
    for d in (1, 3, 2):
        send(f"SX{d}", slab.at[:, mine], slab.at[:, mine], at_x(d))
        send(f"SY{d}", slab.at[:, other], slab.at[:, other], at_x(d))

    sum_across(3)
    sum_across(1)
    for d in range(4):
        sp[:, group(d)] = jnp.transpose(spt[group(d)].astype(F32)).astype(BF16)
    dx_mate(1)
    got_ways("U1")
    add(low(1), sa, sb, [ru1.at[0]], "snd")
    add(high(3), sa, sb, [ru1.at[1]], "snd")
    send("U3+", snd.at[low(1), SB], ru0.at[0, pl.ds(0, half)], at_h(1))
    send("U3-", snd.at[high(3), SB], ru0.at[1, pl.ds(half, half)], at_h(3))
    send("T2+", snd.at[rows(1, mate), SA], rt0.at[0, 1], at_h(1))
    dx_mate(0)
    got_ways("T1")
    add(rows(3, mate), 0, sa, [rt1.at[1]], "snd")
    send("T3-", snd.at[rows(3, mate), SA], rt0.at[1, 1], at_h(3))
    send("T2-", snd.at[rows(3, y), SA], rt0.at[1, 0], at_h(3))
    add(rows(1, y), 0, sa, [rt1.at[0]], "snd")
    send("T3+", snd.at[rows(1, y), SA], rt0.at[0, 0], at_h(1))
    sum_across(0, "dwp")
    dx_own()

    got("SX1", "SX3", "SX2", "SY1", "SY3", "SY2")
    for j in range(8):
        at = block(2 * j + c)
        pltpu.make_async_remote_copy(
            src_ref=slab.at[:, at], dst_ref=slab.at[:, at], send_sem=gsem.at[2], recv_sem=gsem.at[3],
            device_id=at_c, device_id_type=MESH,
        ).start()

    got_ways("U2", "U3")
    add(group(0), sa, sb, [ru0.at[0], ru0.at[1]])
    for k, at in enumerate((near, far)):
        send(f"sb{k}", snd.at[rows(0, at), SB], rb.at[k], link)
    got("T2+", "T3-")
    add(rows(0, mate), 0, sa, [rt0.at[0, 1], rt0.at[1, 1]], "snd")
    send("fa", snd.at[rows(0, mate), SA], rs.at[:, SA], pair)
    got("sb0", "sb1")
    add(rows(0, mate), sa, sb, [rb.at[1]], "snd")
    send("fb", snd.at[rows(0, mate), SB], rs.at[:, SB], pair)
    add(mine_rows, sa, sb, [rb.at[0]], "dwp")
    wg_out[0, :, wide(base + sa, sb)] = dwp[mine_rows, SB]
    got("fa", "fb")
    wg_out[0, :, wide(mate_base, n)] = rs[...].astype(F32)
    got("dx0", "dx1")
    all_blocks(2, slab.at[:, pl.ds(0, slab.shape[1] // 2)]).wait_recv()
    got("T3+", "T2-")
    wg_out[0, :, wide(base, sa)] = dwp[mine_rows, SA] + rt0[0, 0].astype(F32) + rt0[1, 0].astype(F32)

    for copy in copies.values():
        copy.wait_send()
    all_blocks(0, rc).wait_send()
    all_blocks(2, slab.at[:, pl.ds(0, slab.shape[1] // 2)]).wait_send()


def drain(*refs):
    sems = refs[-1]
    moves = [pltpu.make_async_copy(refs[n], refs[5 + n], sems.at[n]) for n in range(5)]
    for move in moves:
        move.start()
    for move in moves:
        move.wait()


def on_device(pseudo_grads, master_slab, momentum, inner_inputs, token_ids, inner_weight, readout):
    groups = lax.axis_size("island")
    tokens, k = inner_inputs.shape
    r = inner_weight.shape[1]
    features = readout.shape[0]
    g = 4 * r
    width, cols = pseudo_grads.shape[2], master_slab.shape[1]
    out_rows = pseudo_grads.shape[1]
    n = k // 2
    share, back_share = 10 * n // 16, 10 * n // 16
    sa, sb = back_share, n - back_share
    scale = 1.0 / math.sqrt(tokens * lax.axis_size("fsdp"))
    V, sem = pltpu.VMEM, pltpu.SemaphoreType.DMA
    anywhere = pl.BlockSpec(memory_space=pl.ANY)

    def body(*refs):
        kernel(groups, share, back_share, scale, *refs)

    shapes = (
        ((out_rows, width), BF16),
        (master_slab.shape, F32),
        (momentum.shape, F32),
        ((1, r, k), F32),
        ((tokens, k), BF16),
    )
    results = pl.pallas_call(
        body,
        out_shape=tuple(V(*shape) for shape in shapes),
        in_specs=[anywhere] * 7,
        out_specs=[pl.BlockSpec(memory_space=pltpu.VMEM)] * 5,
        scratch_shapes=[
            V((tokens, n), BF16),
            V((tokens, n), BF16),
            V((features, n), BF16),
            V((features, n), F32),
            V((features, n), BF16),
            V((features, tokens), BF16),
            V((tokens, features), BF16),
            V((features, tokens), BF16),
            V((tokens, features), BF16),
            V((tokens, n), BF16),
            V((1, tokens), jnp.int32),
            V((4, g), F32),
            V((features, tokens), F32),
            V((features, tokens), F32),
            V((features, tokens), F32),
            V((4, 2, r, sa), BF16),
            V((2, r, sa), BF16),
            V((2, 2, r, sa), BF16),
            V((2, g // 2, sb), BF16),
            V((2, g, sb), BF16),
            V((2, r, sb), BF16),
            V((r, n), BF16),
            V((8, out_rows, cols), F32),
            V((8, out_rows, cols), F32),
            V((3, 2, out_rows, cols), F32),
            V((out_rows, cols), F32),
            V((out_rows, cols), F32),
            V((out_rows, cols), F32),
            sem((N_SEMS,)),
            sem((N_SEMS,)),
            sem((12,)),
            sem((4,)),
        ],
        compiler_params=pltpu.CompilerParams(
            collective_id=0, has_side_effects=True, vmem_limit_bytes=54 * 2**20
        ),
        name="window",
    )(
        pseudo_grads, master_slab, momentum, inner_inputs, token_ids.reshape(1, tokens),
        inner_weight, readout.reshape(4, g),
    )
    return pl.pallas_call(
        drain,
        out_shape=tuple(jax.ShapeDtypeStruct(*shape) for shape in shapes),
        in_specs=[pl.BlockSpec(memory_space=pltpu.VMEM)] * 5,
        out_specs=[anywhere] * 5,
        scratch_shapes=[sem((5,))],
        compiler_params=pltpu.CompilerParams(vmem_limit_bytes=2**20),
        name="drain",
    )(*(pltpu.with_memory_space_constraint(result, pltpu.VMEM) for result in results))


def solution(mesh):
    in_specs = (
        P("island", "fsdp", None),
        P("fsdp", "island"),
        P("fsdp", "island"),
        P(("island", "fsdp"), None),
        P(("island", "fsdp")),
        P("island", "fsdp", None),
        P(),
    )
    out_specs = (
        P("fsdp", None),
        P("fsdp", "island"),
        P("fsdp", "island"),
        P("island", "fsdp", None),
        P(("island", "fsdp"), None),
    )
    return jax.shard_map(
        on_device, mesh=mesh, in_specs=in_specs, out_specs=out_specs, check_vma=False
    )
```

```python
import math

import jax
import jax.numpy as jnp
from jax import lax
from jax.experimental import pallas as pl
from jax.experimental.pallas import tpu as pltpu
from jax.sharding import PartitionSpec as P

MESH = pl.DeviceIdType.MESH
F32, BF16 = jnp.float32, jnp.bfloat16
N_SEMS = 96


def kernel(
    groups, share, back_share, scale,
    pg, master, momentum, xin, tok, w, readout,
    slab, master_out, momentum_out, wg_out, dxb,
    xo, xp, wv, dwp, snd, slt, slo, spt, sp, dxs, tokb, rob, preo, ps, pr,
    ra, rt1, rt0, ru1, ru0, rb, rs,
    acc, rc, rx, rz, msb, mob,
    ssem, rsem, lsem, gsem,
):
    f, i = lax.axis_index("fsdp"), lax.axis_index("island")
    h, y = f // 4, lax.rem(f, 4)
    x, z, c = i // 4, lax.rem(i // 2, 2), lax.rem(i, 2)

    one, two = y + 1 - 2 * lax.rem(y, 2), 3 - y
    mate = one + c * (two - one)
    near = two + c * (one - two)
    far = 3 - one
    n = xo.shape[1]
    side = lax.rem((y + 1) // 2, 2) * (1 - c) + (y // 2) * c
    base, mate_base = n * side, n * (1 - side)

    def at_y(d):
        return {"fsdp": h * 4 + d}

    def at_h(d):
        return {"fsdp": lax.rem(h + d, 4) * 4 + y}

    def at_x(d):
        return {"island": lax.rem(x + d, 4) * 4 + z * 2 + c}

    at_z = {"island": x * 4 + (1 - z) * 2 + c}
    at_c = {"island": x * 4 + z * 2 + 1 - c}
    pair, link = at_y(mate), at_y(near)
    ways = (("+", at_h(1), 3), ("-", at_h(3), 1))

    r = w.shape[1]
    g = r * 4
    half = g // 2
    ca, cb = share, n - share
    A, B = pl.ds(0, ca), pl.ds(ca, cb)
    sa, sb = back_share, n - back_share
    SA, SB = pl.ds(0, sa), pl.ds(sa, sb)

    def rows(dh, at):
        return pl.ds(pl.multiple_of(dh * g + at * r, r), r)

    def group(dh):
        return pl.ds(dh * g, g)

    def low(dh):
        return pl.ds(dh * g, half)

    def high(dh):
        return pl.ds(dh * g + half, half)

    def wide(start, size):
        return pl.ds(pl.multiple_of(start, 128), size)

    def own_w(lo, size):
        return w.at[0, :, wide(base + lo, size)]

    copies = {}

    def send(name, src, dst, device):
        k = len(copies)
        copies[name] = pltpu.make_async_remote_copy(
            src_ref=src, dst_ref=dst, send_sem=ssem.at[k], recv_sem=rsem.at[k],
            device_id=device, device_id_type=MESH,
        )
        copies[name].start()

    def got(*names):
        for name in names:
            copies[name].wait_recv()

    def got_ways(*names):
        for name in names:
            got(name + "+", name + "-")

    def load(src, dst, k):
        cp = pltpu.make_async_copy(src, dst, lsem.at[k])
        cp.start()
        return cp

    cols = slab.shape[1] // groups

    def block(k):
        return wide(k * cols, cols)

    mine_rows = rows(0, y)
    lw = load(own_w(0, n), wv.at[mine_rows], 0)
    lx = load(xin.at[:, wide(base, n)], xo, 1)
    small = [load(tok, tokb, 4), load(readout, rob, 5)]
    states = [load(master, msb, 6), load(momentum, mob, 7)]
    for j in range(8):
        pltpu.make_async_copy(pg.at[0, :, block(2 * j + c)], acc.at[j], lsem.at[8]).start()

    barrier = pltpu.get_barrier_semaphore()
    partners = [pair, link, at_h(1), at_h(3), at_x(1), at_x(2), at_x(3), at_z, at_c]
    for device in partners:
        pl.semaphore_signal(barrier, inc=1, device_id=device, device_id_type=MESH)
    pl.semaphore_wait(barrier, len(partners))

    send("w", w.at[0, :, wide(mate_base, n)], wv.at[mine_rows], pair)
    for s, device, slot in ways:
        send(f"wao{s}", own_w(0, ca), wv.at[rows(slot, y), A], device)
    send("ybo", own_w(ca, cb), wv.at[mine_rows, B], link)
    for j in range(8):
        pltpu.make_async_remote_copy(
            src_ref=pg.at[0, :, block(2 * j + 1 - c)], dst_ref=rc.at[j], send_sem=gsem.at[0], recv_sem=gsem.at[1],
            device_id=at_c, device_id_type=MESH,
        ).start()

    def all_blocks(k, ref):
        return pltpu.make_async_remote_copy(
            src_ref=ref, dst_ref=ref, send_sem=gsem.at[k], recv_sem=gsem.at[k + 1], device_id=at_c, device_id_type=MESH
        )

    def product(at_rows, xs):
        def body(j, total):
            at = wide(j * (n // 4), n // 4)
            return total + lax.dot_general(
                wv[at_rows, at], xs[:, at], (((1,), (1,)), ((), ())), preferred_element_type=F32
            )

        return lax.fori_loop(0, 4, body, jnp.zeros((g, xs.shape[0]), F32))

    def pre_mate(d):
        ps[group(d)] = product(group(d), xp)
        send(f"p{d}", ps.at[group(d)], pr.at[group(d)], pair)

    def pre_own(d):
        preo[group(d)] = product(group(d), xo)

    def slope(d):
        got(f"p{d}")
        p = preo[group(d)] + pr[group(d)]
        sig = jax.nn.sigmoid(p)
        keep = (tokb[...] != 0).astype(F32)
        row = rob[pl.ds(lax.rem(h + d, 4), 1), :]
        column = jnp.transpose(jnp.broadcast_to(row, (g, g)))
        weight = jnp.concatenate([column] * (p.shape[1] // g), axis=1)
        value = scale * keep * weight * (sig * (1.0 + p * (1.0 - sig)))
        slt[group(d)] = value.astype(BF16)
        send(f"s{d}", slt.at[group(d)], spt.at[group(d)], pair)
        slo[:, group(d)] = jnp.transpose(value).astype(BF16)

    def turn(d):
        sp[:, group(d)] = jnp.transpose(spt[group(d)].astype(F32)).astype(BF16)

    def dw(d, wait=True):
        if wait:
            got(f"s{d}")
        own, other = slt[group(d)], spt[group(d)]

        def body(j, carry):
            at = wide(j * (n // 4), n // 4)
            part = jnp.dot(own, xo[:, at], preferred_element_type=F32) + jnp.dot(
                other, xp[:, at], preferred_element_type=F32
            )
            dwp[group(d), at] = part
            snd[group(d), at] = part.astype(BF16)
            return carry

        lax.fori_loop(0, 4, body, 0)

    def add(at_rows, lo, size, terms, to=None):
        units = size // 128
        step = 128 * max(k for k in range(1, 13 if at_rows.size == r else 6) if units % k == 0)

        def body(j, carry):
            at = wide(lo + j * step, step)
            there = wide(j * step, step)
            total = dwp[at_rows, at]
            for ref in terms:
                total = total + ref[:, there].astype(F32)
            if to != "snd":
                dwp[at_rows, at] = total
            if to != "dwp":
                snd[at_rows, at] = total.astype(BF16)
            return carry

        lax.fori_loop(0, size // step, body, 0)

    def across(d, at):
        part = wv.at[rows(d, y if at == "o" else mate), A]
        send(f"ya{d}{at}", part, part, link)

    def across_done(d):
        got(f"ya{d}o", f"ya{d}m")

    def across_back(d):
        for k, at in enumerate((near, far)):
            send(f"sa{d}{k}", snd.at[rows(d, at), SA], ra.at[d, k], link)

    def sum_across(d, to=None):
        got(f"sa{d}0", f"sa{d}1")
        add(rows(d, y), 0, sa, [ra.at[d, 0]], to)
        add(rows(d, mate), 0, sa, [ra.at[d, 1]], to)

    def dx_mate(k):
        def body(j, carry):
            at = wide(k * (n // 2) + j * (n // 4), n // 4)
            dxs[:, at] = jnp.dot(sp[...], wv[:, at], preferred_element_type=F32).astype(BF16)
            return carry

        lax.fori_loop(0, 2, body, 0)
        at = pl.ds(k * (n // 2), n // 2)
        send(f"dx{k}", dxs.at[:, at], dxb.at[:, wide(base + k * (n // 2), n // 2)], pair)

    def dx_own():
        def body(j, carry):
            at = wide(j * (n // 4), n // 4)
            there = wide(base + j * (n // 4), n // 4)
            dxb[:, there] = jnp.dot(slo[...], wv[:, at], preferred_element_type=F32).astype(BF16)
            return carry

        lax.fori_loop(0, 4, body, 0)

    got("w")
    part = wv.at[rows(0, mate), B]
    send("ybm", part, part, link)
    for s, device, slot in ways:
        send(f"wam{s}", wv.at[rows(0, mate), A], wv.at[rows(slot, mate), A], device)
    send("x", xin.at[:, wide(mate_base, n)], xp, pair)
    got("ybo", "ybm")
    lw.wait()
    for s, device, slot in ways:
        send(f"hb{s}", wv.at[group(0), B], wv.at[group(slot), B], device)
    got_ways("wao")
    send("wf+", wv.at[rows(3, y), A], wv.at[rows(2, y), A], at_h(1))
    across(3, "o")
    across(1, "o")
    got_ways("wam")
    send("wf-", wv.at[rows(1, mate), A], wv.at[rows(2, mate), A], at_h(3))
    across(3, "m")
    across(1, "m")

    pltpu.make_async_copy(acc, acc, lsem.at[8]).wait()
    all_blocks(0, rc).wait_recv()
    for j in range(8):
        acc[j] = acc[j] + rc[j]
    for d in (1, 3, 2):
        send(f"X{d}", acc.at[pl.ds(lax.rem(x + d, 4) * 2, 2)], rx.at[d - 1], at_x(d))
    got("X1", "X3", "X2")
    blocks = acc.at[pl.ds(x * 2, 2)]
    blocks[...] = blocks[...] + rx[0] + rx[1] + rx[2]

    lx.wait()
    for cp in small + states:
        cp.wait()
    got_ways("hb")
    send("hbf+", wv.at[low(3), B], wv.at[low(2), B], at_h(1))
    send("hbf-", wv.at[high(1), B], wv.at[high(2), B], at_h(3))
    send("Z", acc.at[x * 2 + 1 - z], rz, at_z)
    across_done(3)
    across_done(1)
    pre_own(3)
    got("x")
    pre_mate(3)
    pre_mate(1)
    got_ways("wf")
    pre_own(1)
    across(2, "m")
    across(2, "o")
    across(0, "m")
    slope(3)
    across(0, "o")
    slope(1)
    dw(3)
    dw(1)
    got_ways("hbf")
    send("U2+", snd.at[high(1), SB], ru0.at[0, pl.ds(half, half)], at_h(1))
    send("U2-", snd.at[low(3), SB], ru0.at[1, pl.ds(0, half)], at_h(3))
    across_done(2)
    pre_mate(2)
    pre_own(2)

    got("Z")
    mean = (acc[x * 2 + z] + rz[...]) / groups
    stepped = 0.9 * mob[...] + mean
    momentum_out[...] = stepped
    master_out[...] = msb[...] - 0.7 * (mean + 0.9 * stepped)
    mine = block(i)
    slab[:, mine] = master_out[...].astype(BF16)
    send("SZ", slab.at[:, mine], slab.at[:, mine], at_z)

    slope(2)
    across_done(0)
    pre_mate(0)
    across_back(1)
    dw(2)
    send("U1+", snd.at[low(2), SB], ru1.at[0], at_h(1))
    send("U1-", snd.at[high(2), SB], ru1.at[1], at_h(3))
    across_back(2)
    across_back(3)
    pre_own(0)
    slope(0)
    for d in (1, 3, 2):
        turn(d)
    sum_across(2)
    send("T1+", snd.at[rows(2, y), SA], rt1.at[0], at_h(1))
    send("T1-", snd.at[rows(2, mate), SA], rt1.at[1], at_h(3))
    got("s0")
    turn(0)
    dx_mate(1)

    got("SZ")
    other = block(x * 4 + (1 - z) * 2 + c)
    for d in (1, 3, 2):
        send(f"SX{d}", slab.at[:, mine], slab.at[:, mine], at_x(d))
        send(f"SY{d}", slab.at[:, other], slab.at[:, other], at_x(d))

    sum_across(1)
    got_ways("U1")
    add(low(1), sa, sb, [ru1.at[0]], "snd")
    add(high(3), sa, sb, [ru1.at[1]], "snd")
    send("U3+", snd.at[low(1), SB], ru0.at[0, pl.ds(0, half)], at_h(1))
    send("U3-", snd.at[high(3), SB], ru0.at[1, pl.ds(half, half)], at_h(3))
    send("T2+", snd.at[rows(1, mate), SA], rt0.at[0, 1], at_h(1))
    dx_mate(0)
    dw(0, False)
    across_back(0)
    sum_across(3)
    got_ways("T1")
    add(rows(3, mate), 0, sa, [rt1.at[1]], "snd")
    send("T3-", snd.at[rows(3, mate), SA], rt0.at[1, 1], at_h(3))
    send("T2-", snd.at[rows(3, y), SA], rt0.at[1, 0], at_h(3))
    add(rows(1, y), 0, sa, [rt1.at[0]], "snd")
    send("T3+", snd.at[rows(1, y), SA], rt0.at[0, 0], at_h(1))
    sum_across(0, "dwp")
    dx_own()

    got("SX1", "SX3", "SX2", "SY1", "SY3", "SY2")
    for j in range(8):
        at = block(2 * j + c)
        pltpu.make_async_remote_copy(
            src_ref=slab.at[:, at], dst_ref=slab.at[:, at], send_sem=gsem.at[2], recv_sem=gsem.at[3],
            device_id=at_c, device_id_type=MESH,
        ).start()

    got_ways("U2", "U3")
    add(group(0), sa, sb, [ru0.at[0], ru0.at[1]])
    for k, at in enumerate((near, far)):
        send(f"sb{k}", snd.at[rows(0, at), SB], rb.at[k], link)
    got("T2+", "T3-")
    add(rows(0, mate), 0, sa, [rt0.at[0, 1], rt0.at[1, 1]], "snd")
    send("fa", snd.at[rows(0, mate), SA], rs.at[:, SA], pair)
    got("sb0", "sb1")
    add(rows(0, mate), sa, sb, [rb.at[1]], "snd")
    send("fb", snd.at[rows(0, mate), SB], rs.at[:, SB], pair)
    add(mine_rows, sa, sb, [rb.at[0]], "dwp")
    wg_out[0, :, wide(base + sa, sb)] = dwp[mine_rows, SB]
    got("fa", "fb")
    wg_out[0, :, wide(mate_base, n)] = rs[...].astype(F32)
    got("dx0", "dx1")
    all_blocks(2, slab.at[:, pl.ds(0, slab.shape[1] // 2)]).wait_recv()
    got("T3+", "T2-")
    wg_out[0, :, wide(base, sa)] = dwp[mine_rows, SA] + rt0[0, 0].astype(F32) + rt0[1, 0].astype(F32)

    for copy in copies.values():
        copy.wait_send()
    all_blocks(0, rc).wait_send()
    all_blocks(2, slab.at[:, pl.ds(0, slab.shape[1] // 2)]).wait_send()


def drain(*refs):
    sems = refs[-1]
    moves = [pltpu.make_async_copy(refs[n], refs[5 + n], sems.at[n]) for n in range(4)]
    part = refs[4].shape[0] // 4
    for n in range(4):
        at = pl.ds(n * part, part)
        moves.insert(n, pltpu.make_async_copy(refs[4].at[at], refs[9].at[at], sems.at[4 + n]))
    for move in moves:
        move.start()
    for move in moves:
        move.wait()


def on_device(pseudo_grads, master_slab, momentum, inner_inputs, token_ids, inner_weight, readout):
    groups = lax.axis_size("island")
    tokens, k = inner_inputs.shape
    r = inner_weight.shape[1]
    features = readout.shape[0]
    g = 4 * r
    width, cols = pseudo_grads.shape[2], master_slab.shape[1]
    out_rows = pseudo_grads.shape[1]
    n = k // 2
    share, back_share = 10 * n // 16, 21 * n // 32
    sa, sb = back_share, n - back_share
    scale = 1.0 / math.sqrt(tokens * lax.axis_size("fsdp"))
    V, sem = pltpu.VMEM, pltpu.SemaphoreType.DMA
    anywhere = pl.BlockSpec(memory_space=pl.ANY)

    def body(*refs):
        kernel(groups, share, back_share, scale, *refs)

    shapes = (
        ((out_rows, width), BF16),
        (master_slab.shape, F32),
        (momentum.shape, F32),
        ((1, r, k), F32),
        ((tokens, k), BF16),
    )
    results = pl.pallas_call(
        body,
        out_shape=tuple(V(*shape) for shape in shapes),
        in_specs=[anywhere] * 7,
        out_specs=[pl.BlockSpec(memory_space=pltpu.VMEM)] * 5,
        scratch_shapes=[
            V((tokens, n), BF16),
            V((tokens, n), BF16),
            V((features, n), BF16),
            V((features, n), F32),
            V((features, n), BF16),
            V((features, tokens), BF16),
            V((tokens, features), BF16),
            V((features, tokens), BF16),
            V((tokens, features), BF16),
            V((tokens, n), BF16),
            V((1, tokens), jnp.int32),
            V((4, g), F32),
            V((features, tokens), F32),
            V((features, tokens), F32),
            V((features, tokens), F32),
            V((4, 2, r, sa), BF16),
            V((2, r, sa), BF16),
            V((2, 2, r, sa), BF16),
            V((2, g // 2, sb), BF16),
            V((2, g, sb), BF16),
            V((2, r, sb), BF16),
            V((r, n), BF16),
            V((8, out_rows, cols), F32),
            V((8, out_rows, cols), F32),
            V((3, 2, out_rows, cols), F32),
            V((out_rows, cols), F32),
            V((out_rows, cols), F32),
            V((out_rows, cols), F32),
            sem((N_SEMS,)),
            sem((N_SEMS,)),
            sem((12,)),
            sem((4,)),
        ],
        compiler_params=pltpu.CompilerParams(
            collective_id=0, has_side_effects=True, vmem_limit_bytes=54 * 2**20
        ),
        name="window",
    )(
        pseudo_grads, master_slab, momentum, inner_inputs, token_ids.reshape(1, tokens),
        inner_weight, readout.reshape(4, g),
    )
    return pl.pallas_call(
        drain,
        out_shape=tuple(jax.ShapeDtypeStruct(*shape) for shape in shapes),
        in_specs=[pl.BlockSpec(memory_space=pltpu.VMEM)] * 5,
        out_specs=[anywhere] * 5,
        scratch_shapes=[sem((8,))],
        compiler_params=pltpu.CompilerParams(vmem_limit_bytes=2**20),
        name="drain",
    )(*(pltpu.with_memory_space_constraint(result, pltpu.VMEM) for result in results))


def solution(mesh):
    in_specs = (
        P("island", "fsdp", None),
        P("fsdp", "island"),
        P("fsdp", "island"),
        P(("island", "fsdp"), None),
        P(("island", "fsdp")),
        P("island", "fsdp", None),
        P(),
    )
    out_specs = (
        P("fsdp", None),
        P("fsdp", "island"),
        P("fsdp", "island"),
        P("island", "fsdp", None),
        P(("island", "fsdp"), None),
    )
    return jax.shard_map(
        on_device, mesh=mesh, in_specs=in_specs, out_specs=out_specs, check_vma=False
    )
```
